32 devices in a mesh: grp: 2 (over y), tp: 4 (over z), ffn: 4 (over x, core).
Axes of the slice: x: 2, y: 2, z: 4, core: 2. Of those that a mesh axis runs over, the one named last changes fastest.
Arguments:
- queries: bfloat16 [192, 8192], P('grp', 'tp'), may hold values from -320 to 320
- new_kv: bfloat16 [2, 192, 1024], P(None, 'grp', 'tp'), may hold values from -12 to 12
- kv_cache: bfloat16 [2, 2, 8192, 1024], P(None, 'grp', 'ffn', 'tp'), may hold values from -12 to 12
- lengths: int32 [2], P('grp'), may hold values from 1 to 96, as said below
- prefixes: int32 [2], P('grp'), may hold values from 0 to 8192, as said below
- resid: bfloat16 [192, 8192], P('grp', 'ffn'), may hold values from -0.29882812 to 0.29882812
- out_weight: bfloat16 [8192, 8192], P('tp', 'ffn'), may hold values from -0.0625 to 0.0625
- gain: bfloat16 [8192], P('ffn'), may hold values from 0.099609375 to 1.8984375
- gate_weight: bfloat16 [8192, 29568], P('ffn', ('grp', 'tp')), may hold values from -0.0625 to 0.0625
- up_weight: bfloat16 [8192, 29568], P('ffn', ('grp', 'tp')), may hold values from -0.0625 to 0.0625
- down_weight: bfloat16 [29568, 8192], P(('grp', 'tp'), 'ffn'), may hold values from -0.03125 to 0.03125
Outputs:
- layer_out: bfloat16 [192, 8192], P(('grp', 'tp'), 'ffn')
The draws below stay inside these ranges and needn't reach their ends.
Inputs may be any that keep to these rules, and one draw needn't show every extreme that they name: `lengths`: some group has a full block of 96 live slots. `prefixes`: some group has all 8192 cached positions in use.
All inputs are finite; a program needn't handle non-finite values.
Results may differ from the reference program's by a relative error of at most 0.02.
Values may be sent and summed in bfloat16 or wider, within the bound.
No kernel may reach another device: no remote copies, remote signals or barrier semaphores. Data moves between devices by JAX's collectives and lax.ppermute only.
A program may use at most 128 MiB of HBM per device.

```python
import jax
import jax.numpy as jnp
from jax import lax

D = 8192
HQ = 64
KVH = 8
DH = 128
FF = 29568
SPAN = 96
TOKENS = 192
CACHE = 8192
N_GRP = 2


def on_grid(values):
    return jnp.floor(values * 16.0) / 16.0


def draw_queries(key, part):
    values = on_grid(jnp.clip(jax.random.normal(key, (TOKENS, HQ * DH), jnp.float32), -5.0, 5.0))
    return values.astype(jnp.bfloat16)


def draw_new_kv(key, part):
    values = 2.0 * jax.random.normal(jax.random.fold_in(key, 31), (2, TOKENS, KVH * DH), jnp.float32)
    return on_grid(jnp.clip(values, -11.9, 11.9)).astype(jnp.bfloat16)


def draw_kv_cache(key, part):
    values = 2.0 * jax.random.normal(jax.random.fold_in(key, 37), (2, N_GRP, CACHE, KVH * DH), jnp.float32)
    return on_grid(jnp.clip(values, -11.9, 11.9)).astype(jnp.bfloat16)


def draw_lengths(key, part):
    first, second = jax.random.split(jax.random.fold_in(key, 11))
    values = jax.random.randint(first, (N_GRP,), 1, SPAN + 1, dtype=jnp.int32)
    spot = jax.random.randint(second, (), 0, N_GRP, dtype=jnp.int32)
    return values.at[spot].set(SPAN)


def draw_prefixes(key, part):
    first, second = jax.random.split(jax.random.fold_in(key, 23))
    values = jax.random.randint(first, (N_GRP,), 0, CACHE + 1, dtype=jnp.int32)
    spot = jax.random.randint(second, (), 0, N_GRP, dtype=jnp.int32)
    return values.at[spot].set(CACHE)


def steps_of(stream_key, shape, pieces, smallest, high):
    def one(dim, blocks):
        steps = jax.random.uniform(jax.random.fold_in(jax.random.fold_in(stream_key, 6), dim), (blocks,), jnp.float32, smallest / len(pieces), high / len(pieces))
        return jnp.repeat(jnp.exp(steps), shape[dim] // blocks).reshape((-1,) + (1,) * (len(shape) - dim - 1))

    factor_of = one(*pieces[0])
    for cut in pieces[1:]:
        factor_of = factor_of * one(*cut)
    return factor_of


def gaussian(key, shape, scale, bound, cuts=(), held_as=jnp.bfloat16):
    entries = jax.random.normal(key, shape, jnp.float32) * scale
    if len(cuts) > 0:
        entries = steps_of(key, shape, cuts, -0.22, 0.18) * entries
    return jnp.clip(entries, min=-bound, max=bound).astype(held_as)


def setup_inputs(seed: int = 0) -> dict:
    seeds = jax.random.split(jax.random.key(seed), 12)
    queries = draw_queries(jax.random.fold_in(seeds[11], 71), 0)
    new_kv = draw_new_kv(jax.random.fold_in(seeds[11], 71), 0)
    kv_cache = draw_kv_cache(jax.random.fold_in(seeds[11], 71), 0)
    lengths = draw_lengths(jax.random.fold_in(seeds[11], 71), 0)
    prefixes = draw_prefixes(jax.random.fold_in(seeds[11], 71), 0)
    resid = gaussian(seeds[5], (TOKENS, D), 0.05, 0.29882812, ((0, 2), (1, 4)))
    out_weight = gaussian(seeds[6], (HQ * DH, D), (HQ * DH) ** -0.5, 0.0625, ((0, 4), (1, 4)))
    gain = jnp.clip(1.0 + 0.18 * jax.random.normal(seeds[7], (D,), jnp.float32), 0.099609375, 1.8984375).astype(jnp.bfloat16)
    gate_weight = gaussian(seeds[8], (D, FF), D ** -0.5, 0.0625, ((0, 4), (1, 8)))
    up_weight = gaussian(seeds[9], (D, FF), D ** -0.5, 0.0625, ((0, 4), (1, 8)))
    down_weight = gaussian(seeds[10], (FF, D), FF ** -0.5, 0.03125, ((0, 8), (1, 4)))
    return {"queries": queries, "new_kv": new_kv, "kv_cache": kv_cache, "lengths": lengths, "prefixes": prefixes, "resid": resid, "out_weight": out_weight, "gain": gain, "gate_weight": gate_weight, "up_weight": up_weight, "down_weight": down_weight}


def attend_group(items):
    q_grp, kn_grp, vn_grp, kc_grp, vc_grp, length, prefix = items
    key_pos = jnp.arange(CACHE + SPAN, dtype=jnp.int32)[None, :]
    row_pos = jnp.arange(SPAN, dtype=jnp.int32)[:, None]
    new_pos = key_pos - CACHE
    valid = jnp.where(key_pos < CACHE, key_pos < prefix, (new_pos < length) & (new_pos <= row_pos))

    def attend_head(parts):
        q_head, kn_head, vn_head, kc_head, vc_head = parts
        keys = jnp.concatenate([kc_head.astype(jnp.float32), kn_head], axis=0)
        values = jnp.concatenate([vc_head.astype(jnp.float32), vn_head], axis=0)
        scores = jnp.einsum('gid,kd->gik', q_head, keys) / jnp.sqrt(jnp.float32(DH))
        scores = jnp.where(valid[None], scores, jnp.float32(-1e+30))
        top = lax.optimization_barrier(jnp.max(scores, axis=-1, keepdims=True))
        probs = jnp.where(valid[None], jnp.exp(scores - top), jnp.float32(0.0))
        total = lax.optimization_barrier(jnp.sum(probs, axis=-1, keepdims=True))
        return jnp.einsum('gik,kd->gid', probs, values) / total
    return lax.map(attend_head, (q_grp, kn_grp, vn_grp, kc_grp, vc_grp))

def reference(queries, new_kv, kv_cache, lengths, prefixes, resid, out_weight, gain, gate_weight, up_weight, down_weight):
    group = HQ // KVH
    q_all = queries.astype(jnp.float32).reshape(N_GRP, SPAN, KVH, group, DH).transpose(0, 2, 3, 1, 4)
    kn_all = new_kv[0].astype(jnp.float32).reshape(N_GRP, SPAN, KVH, DH).transpose(0, 2, 1, 3)
    vn_all = new_kv[1].astype(jnp.float32).reshape(N_GRP, SPAN, KVH, DH).transpose(0, 2, 1, 3)
    kc_all = kv_cache[0].reshape(N_GRP, CACHE, KVH, DH).transpose(0, 2, 1, 3)
    vc_all = kv_cache[1].reshape(N_GRP, CACHE, KVH, DH).transpose(0, 2, 1, 3)
    heads = lax.map(attend_group, (q_all, kn_all, vn_all, kc_all, vc_all, lengths, prefixes))
    attn = heads.transpose(0, 3, 1, 2, 4).reshape(TOKENS, HQ * DH).astype(jnp.bfloat16)
    h1 = (jnp.dot(attn, out_weight, preferred_element_type=jnp.float32) + resid.astype(jnp.float32)).astype(jnp.bfloat16)
    h1f = h1.astype(jnp.float32)
    squares = lax.optimization_barrier(jnp.sum(h1f * h1f, axis=1))
    inv_rms = lax.rsqrt(squares / D + 1e-06)
    scaled = (h1f * gain.astype(jnp.float32)[None, :]).astype(jnp.bfloat16)
    gate = jnp.dot(scaled, gate_weight, preferred_element_type=jnp.float32) * inv_rms[:, None]
    upper = jnp.dot(scaled, up_weight, preferred_element_type=jnp.float32) * inv_rms[:, None]
    hidden = (jax.nn.silu(gate) * upper).astype(jnp.bfloat16)
    down = jnp.dot(hidden, down_weight, preferred_element_type=jnp.float32)
    slot = jnp.arange(TOKENS, dtype=jnp.int32) % SPAN
    live = slot < jnp.repeat(lengths, SPAN)
    return jnp.where(live[:, None], h1f + down, jnp.float32(0.0)).astype(jnp.bfloat16)
```

```python
import functools
import math

import jax
import jax.numpy as jnp
from jax import lax
from jax.experimental import pallas as pl
from jax.experimental.pallas import tpu as pltpu
from jax.sharding import PartitionSpec as P

DH = 128
TILE = 256
NEGATIVE = -1e30
BF16 = jnp.bfloat16
F32 = jnp.float32
LIMIT = 50 * 1024 * 1024
ORDER = (0, 2, 1, 3)


def swapped_bits(index):
    return (index & 1) * 2 + (index >> 1)


def params(limit=LIMIT):
    return pltpu.CompilerParams(vmem_limit_bytes=limit)


def cost(flops, moved, exps=0):
    return pl.CostEstimate(flops=int(flops), bytes_accessed=int(moved), transcendentals=int(exps))


def whole(shape):
    return pl.BlockSpec(shape, lambda *unused: (0,) * len(shape))


def attention_kernel(heads, scalars, q_ref, key_ref, value_ref, new_key_ref, new_value_ref, out_ref, lse_ref, columns):
    step = pl.program_id(0)
    span = q_ref.shape[0]
    cache_len = key_ref.shape[2]
    usable, length, first = scalars[1], scalars[2], scalars[3]
    scale = 1.0 / math.sqrt(DH)
    q = jnp.concatenate([q_ref[:, h * DH : (h + 1) * DH] for h in range(heads)], axis=0)
    contract = (((1,), (1,)), ((), ()))
    scores = lax.dot_general(q, key_ref[0, 0], contract, preferred_element_type=F32)
    position = lax.broadcasted_iota(jnp.int32, (1, cache_len), 1)
    bias = jnp.where(position < usable, 0.0, NEGATIVE)
    scores = scores * scale + bias
    fresh = lax.dot_general(q, new_key_ref[0], contract, preferred_element_type=F32)
    row = lax.broadcasted_iota(jnp.int32, (span, span), 0)
    col = lax.broadcasted_iota(jnp.int32, (span, span), 1)
    allowed = (col <= row) & (col < length) & (first > 0)
    fresh_bias = jnp.where(allowed, 0.0, NEGATIVE)
    fresh = fresh * scale + jnp.concatenate([fresh_bias] * heads, axis=0)
    top = jnp.maximum(
        jnp.max(scores, axis=1, keepdims=True), jnp.max(fresh, axis=1, keepdims=True)
    )
    probs = jnp.exp(scores - top)
    fresh_probs = jnp.exp(fresh - top)
    total = jnp.sum(probs, axis=1, keepdims=True) + jnp.sum(fresh_probs, axis=1, keepdims=True)
    values = jnp.dot(probs.astype(BF16), value_ref[0, 0], preferred_element_type=F32)
    values += jnp.dot(fresh_probs.astype(BF16), new_value_ref[0], preferred_element_type=F32)
    values = (values / total).astype(BF16)
    lse = top + jnp.log(total)
    for h in range(heads):
        out_ref[:, h * DH : (h + 1) * DH] = values[h * span : (h + 1) * span]

    @pl.when(step == 0)
    def first_step():
        columns[...] = jnp.zeros_like(columns)

    lane = lax.broadcasted_iota(jnp.int32, (span, 128), 1)
    kept = columns[0:span, :]
    for h in range(heads):
        kept = jnp.where(lane == step * heads + h, lse[h * span : (h + 1) * span], kept)
    columns[0:span, :] = kept

    @pl.when(step == pl.num_programs(0) - 1)
    def last_step():
        lse_ref[...] = jnp.transpose(columns[...])[0 : lse_ref.shape[0], :]


def attention(scalars, queries, kv_cache, new_kv, local_kv):
    span, qcols = queries.shape
    per_kv = qcols // DH // local_kv
    heads = 4
    steps = per_kv // heads
    cache_len = kv_cache.shape[2]
    width = heads * DH
    call = pl.pallas_call(
        functools.partial(attention_kernel, heads),
        grid_spec=pltpu.PrefetchScalarGridSpec(
            num_scalar_prefetch=1,
            grid=(steps,),
            in_specs=[
                pl.BlockSpec((span, width), lambda i, s: (0, s[0] * steps + i)),
                pl.BlockSpec((1, 1, cache_len, DH), lambda i, s: (0, 0, 0, s[0])),
                pl.BlockSpec((1, 1, cache_len, DH), lambda i, s: (1, 0, 0, s[0])),
                pl.BlockSpec((1, span, DH), lambda i, s: (0, 0, s[0])),
                pl.BlockSpec((1, span, DH), lambda i, s: (1, 0, s[0])),
            ],
            out_specs=[
                pl.BlockSpec((span, width), lambda i, s: (0, i)),
                pl.BlockSpec((per_kv, 128), lambda i, s: (0, 0)),
            ],
            scratch_shapes=[pltpu.VMEM((128, 128), F32)],
        ),
        out_shape=[
            jax.ShapeDtypeStruct((span, per_kv * DH), BF16),
            jax.ShapeDtypeStruct((per_kv, 128), F32),
        ],
        compiler_params=params(60 * 1024 * 1024),
        cost_estimate=cost(
            4 * span * per_kv * cache_len * DH, 4 * cache_len * DH, span * per_kv * cache_len
        ),
    )
    return call(scalars, queries, kv_cache, kv_cache, new_kv, new_kv)


def combine_kernel(a_ref, b_ref, lse_a_ref, lse_b_ref, out_ref, lse_ref):
    span = a_ref.shape[0]
    heads = lse_a_ref.shape[0]
    lse_a, lse_b = lse_a_ref[...], lse_b_ref[...]
    top = jnp.maximum(lse_a, lse_b)
    left, right = jnp.exp(lse_a - top), jnp.exp(lse_b - top)
    total = left + right
    lse_ref[...] = top + jnp.log(total)
    rest = jnp.zeros((128 - 2 * heads, 128), F32)
    table = jnp.transpose(jnp.concatenate([left / total, right / total, rest], axis=0))
    for h in range(heads):
        cols = slice(h * DH, (h + 1) * DH)
        mixed = a_ref[:, cols].astype(F32) * table[0:span, h : h + 1]
        mixed += b_ref[:, cols].astype(F32) * table[0:span, heads + h : heads + h + 1]
        out_ref[:, cols] = mixed.astype(BF16)


def combine(a, b, lse_a, lse_b):
    return pl.pallas_call(
        combine_kernel,
        out_shape=[
            jax.ShapeDtypeStruct(a.shape, BF16),
            jax.ShapeDtypeStruct(lse_a.shape, F32),
        ],
        compiler_params=params(),
        cost_estimate=cost(4 * a.size, 6 * a.size),
    )(a, b, lse_a, lse_b)


def project_kernel(scalars, keep_ref, other_ref, weight_ref, *rest):
    outs, acc = rest[:-1], rest[-1]
    step = pl.program_id(0)
    depth = weight_ref.shape[0]
    half = pl.num_programs(0) // 2
    rows = outs[0].shape[0]

    @pl.when(step < half)
    def from_keep():
        start = pl.multiple_of(step * depth, depth)
        term = jnp.dot(keep_ref[:, pl.ds(start, depth)], weight_ref[...], preferred_element_type=F32)

        @pl.when(step == 0)
        def begin():
            acc[...] = term

        @pl.when(step > 0)
        def go_on():
            acc[...] += term

    @pl.when(step >= half)
    def from_other():
        start = pl.multiple_of((step - half) * depth, depth)
        acc[...] += jnp.dot(
            other_ref[:, pl.ds(start, depth)], weight_ref[...], preferred_element_type=F32
        )

    @pl.when(step == pl.num_programs(0) - 1)
    def finish():
        for k, out in enumerate(outs):
            start = pl.multiple_of((scalars[1] ^ k) * rows, 8)
            out[...] = acc[pl.ds(start, rows), :].astype(out.dtype)


def project(scalars, keep, other, out_weight, tp_size):
    span, width = keep.shape
    depth = 512
    half = width // depth
    cols = out_weight.shape[1]
    rows = span // tp_size
    return pl.pallas_call(
        project_kernel,
        grid_spec=pltpu.PrefetchScalarGridSpec(
            num_scalar_prefetch=1,
            grid=(2 * half,),
            in_specs=[
                whole((span, width)),
                whole((span, width)),
                pl.BlockSpec(
                    (depth, cols),
                    lambda i, s: (jnp.where(i < half, s[0], 1 - s[0]) * half + i % half, 0),
                ),
            ],
            out_specs=[whole((rows, cols))] * tp_size,
            scratch_shapes=[pltpu.VMEM((span, cols), F32)],
        ),
        out_shape=[
            jax.ShapeDtypeStruct((rows, cols), F32 if k == 0 else BF16) for k in range(tp_size)
        ],
        compiler_params=params(),
        cost_estimate=cost(4 * span * width * cols, 4 * width * cols),
    )(scalars, keep, other, out_weight)


def scale_kernel(slots, scalars, *refs):
    count = 4 * slots
    sources, gain_ref, scaled_ref, square_ref = refs[:count], refs[count], refs[count + 1], refs[count + 2]
    gain = gain_ref[...].astype(F32)
    cols = gain.shape[1]
    for k in range(4):
        place = swapped_bits(scalars[0] ^ k)
        rows = jnp.concatenate(
            [sources[k * slots + s][...].astype(F32) for s in range(slots)], axis=0
        )
        scaled_ref[place] = (rows * gain).astype(BF16)
        squares = rows * rows
        part = squares[:, 0:128]
        for c in range(128, cols, 128):
            part += squares[:, c : c + 128]
        square_ref[place] = part


def scale_rows(scalars, sources, gain):
    slots = len(sources) // 4
    rows, cols = sources[0].shape
    high = rows * slots
    return pl.pallas_call(
        functools.partial(scale_kernel, slots),
        grid_spec=pltpu.PrefetchScalarGridSpec(
            num_scalar_prefetch=1,
            grid=(1,),
            in_specs=[whole((rows, cols))] * len(sources) + [whole((1, cols))],
            out_specs=[whole((4, high, cols)), whole((4, high, 128))],
        ),
        out_shape=[
            jax.ShapeDtypeStruct((4, high, cols), BF16),
            jax.ShapeDtypeStruct((4, high, 128), F32),
        ],
        compiler_params=params(),
        cost_estimate=cost(4 * 4 * high * cols, 4 * 4 * high * cols),
    )(scalars, *sources, gain)


def gate_up_kernel(scaled_ref, gate_ref, up_ref, keep_ref, cross_ref, send_ref):
    places, high, depth = scaled_ref.shape
    rows = scaled_ref[...].reshape(places * high, depth)
    for which, weight in enumerate((gate_ref, up_ref)):
        term = lax.dot_general(
            rows, weight[...], (((1,), (1,)), ((), ())), preferred_element_type=F32
        ).astype(BF16)
        keep_ref[which] = term[0:high]
        cross_ref[which] = term[high : 2 * high]
        send_ref[0, which] = term[2 * high : 3 * high]
        send_ref[1, which] = term[3 * high :]


def gate_up(scaled, gate_weight, up_weight, begin, width):
    places, high, depth = scaled.shape
    tiles = pl.cdiv(width, TILE)
    first = begin // TILE
    weight = pl.BlockSpec((TILE, depth), lambda j: (first + j, 0))
    piece = pl.BlockSpec((2, high, TILE), lambda j: (0, 0, j))
    return pl.pallas_call(
        gate_up_kernel,
        grid=(tiles,),
        in_specs=[whole(scaled.shape), weight, weight],
        out_specs=[piece, piece, pl.BlockSpec((2, 2, high, TILE), lambda j: (0, 0, 0, j))],
        out_shape=[
            jax.ShapeDtypeStruct((2, high, width), BF16),
            jax.ShapeDtypeStruct((2, high, width), BF16),
            jax.ShapeDtypeStruct((2, 2, high, width), BF16),
        ],
        compiler_params=params(),
        cost_estimate=cost(4 * places * high * depth * width, 4 * depth * width),
    )(scaled, gate_weight, up_weight)


def down_kernel(width, slots, has_start, last, scalars, *refs):
    hidden = refs[0:4]
    weight_ref = refs[4]
    rest = list(refs[5:])
    start_ref = rest.pop(0) if has_start else None
    acc, packed = rest[-2], rest[-1]
    outs = rest[:-2]
    step = pl.program_id(0)
    depth = weight_ref.shape[0]
    high = hidden[0].shape[0]
    steps = pl.num_programs(0)

    @pl.when(step == 0)
    def begin():
        if width % depth:
            packed[...] = jnp.zeros_like(packed)
        for place in range(4):
            packed[place * high : (place + 1) * high, 0:width] = hidden[place][...]
        if has_start:
            acc[...] = start_ref[...]
        else:
            acc[...] = jnp.zeros_like(acc)

    start = pl.multiple_of(step * depth, depth)

    def add(weight):
        term = jnp.dot(packed[:, pl.ds(start, depth)], weight, preferred_element_type=F32)
        acc[...] += term.reshape(acc.shape)

    if width % depth:

        @pl.when(step < steps - 1)
        def inner():
            add(weight_ref[...])

        @pl.when(step == steps - 1)
        def edge():
            row = lax.broadcasted_iota(jnp.int32, weight_ref.shape, 0)
            add(jnp.where(row < width % depth, weight_ref[...], jnp.zeros_like(weight_ref)))
    else:
        add(weight_ref[...])

    @pl.when(step == steps - 1)
    def finish():
        if not last:
            outs[0][...] = acc[...]
            return
        rows = high // slots
        for k in range(4):
            place = swapped_bits(scalars[0] ^ k)
            block = acc[place]
            for s in range(slots):
                out = outs[k * slots + s]
                out[...] = block[s * rows : (s + 1) * rows].astype(out.dtype)


def down(scalars, hidden, down_weight, begin, start, slots, last):
    high, width = hidden[0].shape
    cols = down_weight.shape[1]
    steps = pl.cdiv(width, TILE)
    first = begin // TILE
    rows = high // slots
    ins = [whole((high, width))] * 4 + [pl.BlockSpec((TILE, cols), lambda i, s: (first + i, 0))]
    args = list(hidden) + [down_weight]
    if start is not None:
        ins.append(whole((4, high, cols)))
        args.append(start)
    if last:
        shapes = [
            jax.ShapeDtypeStruct((rows, cols), F32 if s == 0 else BF16)
            for k in range(4)
            for s in range(slots)
        ]
    else:
        shapes = [jax.ShapeDtypeStruct((4, high, cols), F32)]
    return pl.pallas_call(
        functools.partial(down_kernel, width, slots, start is not None, last),
        grid_spec=pltpu.PrefetchScalarGridSpec(
            num_scalar_prefetch=1,
            grid=(steps,),
            in_specs=ins,
            out_specs=[whole(shape.shape) for shape in shapes],
            scratch_shapes=[
                pltpu.VMEM((4, high, cols), F32),
                pltpu.VMEM((4 * high, steps * TILE), BF16),
            ],
        ),
        out_shape=shapes,
        compiler_params=params(),
        cost_estimate=cost(8 * high * width * cols, 2 * width * cols),
    )(scalars, *args)


def to_core(x):
    return lax.ppermute(x, "ffn", [(i, i ^ 1) for i in range(4)])


def to_x(x):
    return lax.ppermute(x, "ffn", [(i, i ^ 2) for i in range(4)])


def to_z(x, k):
    return lax.ppermute(x, "tp", [(i, i ^ k) for i in range(4)])


def to_y(x):
    return lax.ppermute(x, "grp", [(0, 1), (1, 0)])


def cut(total):
    tiles = -(-total // TILE)
    head = (tiles + 1) // 2 * TILE
    return [(0, head), (head, total - head)]


def body(
    queries,
    new_kv,
    kv_cache,
    lengths,
    prefixes,
    resid,
    out_weight,
    gain,
    gate_weight,
    up_weight,
    down_weight,
):
    span = queries.shape[0]
    local_kv = new_kv.shape[2] // DH
    cache_len = kv_cache.shape[2]
    groups = lax.axis_size("grp")
    tp_size = lax.axis_size("tp")
    g, t, f = lax.axis_index("grp"), lax.axis_index("tp"), lax.axis_index("ffn")
    core = f & 1
    length = lengths[0]
    rows = span // tp_size
    model = gain.shape[0] * lax.axis_size("ffn")
    usable = jnp.clip(prefixes[0] - f * cache_len, 0, cache_len)
    first = (f == 0).astype(jnp.int32)

    def attend(which):
        scalars = jnp.stack([which, usable, length, first]).astype(jnp.int32)
        return attention(scalars, queries, kv_cache, new_kv, local_kv)

    sent, sent_lse = attend(1 - core)
    got, got_lse = to_core(sent), to_core(sent_lse)
    kept, kept_lse = attend(core)
    kept, kept_lse = combine(kept, got, kept_lse, got_lse)
    got, got_lse = to_x(kept), to_x(kept_lse)
    mine, unused = combine(kept, got, kept_lse, got_lse)
    other = to_core(mine)

    order = jnp.stack([core, t]).astype(jnp.int32)
    terms = project(order, mine, other, out_weight, tp_size)
    own_resid = lax.dynamic_slice_in_dim(resid, t * rows, rows, 0).astype(F32)
    summed = terms[0] + own_resid
    for k in (1, 3, 2):
        summed += to_z(terms[k], k).astype(F32)
    h1 = summed.astype(BF16)

    turn = jnp.stack([t ^ f]).astype(jnp.int32)
    natural = g ^ jnp.arange(groups, dtype=jnp.int32)
    by_z = [h1, to_z(h1, 1), to_z(h1, 2), to_z(h1, 3)]
    sources = []
    for part in by_z:
        if groups == 2:
            sources += [part, to_y(part)]
        else:
            everyone = jnp.take(lax.all_gather(part, "grp"), natural, axis=0)
            sources += [everyone[s] for s in range(groups)]
    scaled, squares = scale_rows(turn, sources, gain[None, :])

    pair = squares[0:2] + to_core(squares[2:4])
    own_squares = pair[0] + to_x(pair[1])
    inv_rms = lax.rsqrt(jnp.sum(own_squares, axis=1, keepdims=True) / model + 1e-06)

    chunks = cut(gate_weight.shape[1])
    total = None
    parts = [gate_up(scaled, gate_weight.T, up_weight.T, begin, width) for begin, width in chunks]
    for index, (begin, width) in enumerate(chunks):
        keep, cross, send = parts[index]
        got = to_core(send)
        crossed = to_x((cross.astype(F32) + got[1].astype(F32)).astype(BF16))
        both = (keep.astype(F32) + got[0].astype(F32) + crossed.astype(F32)) * inv_rms
        hidden = (jax.nn.silu(both[0]) * both[1]).astype(BF16)
        over = to_x(hidden)
        pieces = [hidden, over, to_core(hidden), to_core(over)]
        is_last = index == len(chunks) - 1
        result = down(turn, pieces, down_weight, begin, total, groups, is_last)
        total = None if is_last else result[0]

    chunk_sums = []
    for k in range(4):
        own = result[k * groups]
        others = result[k * groups + 1 : (k + 1) * groups]
        if groups == 2:
            chunk_sums.append((own, others[0]))
        else:
            stacked = jnp.stack([own.astype(BF16)] + list(others))
            stacked = jnp.take(stacked, natural, axis=0)
            moved = lax.all_to_all(stacked, "grp", split_axis=0, concat_axis=0, tiled=True)
            chunk_sums.append(jnp.sum(moved.astype(F32), axis=0))
    out = h1.astype(F32)
    for k in (3, 2, 1, 0):
        if groups == 2:
            own, away = chunk_sums[k]
            value = own + to_y(away).astype(F32)
        else:
            value = chunk_sums[k]
        out += value if k == 0 else to_z(value.astype(BF16), k).astype(F32)
    live = t * rows + jnp.arange(rows, dtype=jnp.int32) < length
    return jnp.where(live[:, None], out, 0.0).astype(BF16)


def merged(x, axis, combine):
    everything = jax.tree.map(lambda part: lax.all_gather(part, axis), x)
    leading = jax.tree.map(lambda part: part[0], everything)

    def hop(k, so_far):
        return combine(so_far, jax.tree.map(lambda part: part[k], everything))

    return lax.fori_loop(1, lax.axis_size(axis), hop, leading)


def combine_parts(first, second):
    top = jnp.maximum(first[0], second[0])
    left = jnp.exp(first[0] - top)
    right = jnp.exp(second[0] - top)
    total = first[1] * left + second[1] * right
    values = first[2] * left[..., None] + second[2] * right[..., None]
    return (top, total, values)


def general_body(
    queries,
    new_kv,
    kv_cache,
    lengths,
    prefixes,
    resid,
    out_weight,
    gain,
    gate_weight,
    up_weight,
    down_weight,
):
    span, qcols = queries.shape
    kcols = new_kv.shape[2]
    local_kv = kcols // DH
    group = qcols // DH // local_kv
    cache_len = kv_cache.shape[2]
    length = lengths[0]
    model = gain.shape[0] * lax.axis_size("ffn")
    prefix = prefixes[0]
    width_index = lax.axis_index("ffn")
    shard_start = width_index * cache_len
    query_heads = (
        queries.reshape(span, local_kv, group, DH)
        .transpose(1, 2, 0, 3)
        .reshape(local_kv, group * span, DH)
    )
    row_pos = jnp.tile(jnp.arange(span, dtype=jnp.int32), group)
    inv_scale = 1.0 / math.sqrt(DH)

    def update(state, keys, values, valid):
        top, total, acc = state
        scores = (
            jnp.einsum("hrd,hkd->hrk", query_heads, keys, preferred_element_type=jnp.float32)
            * inv_scale
        )
        scores = jnp.where(valid[None], scores, NEGATIVE)
        new_top = jnp.maximum(top, jnp.max(scores, axis=-1))
        probs = jnp.where(valid[None], jnp.exp(scores - new_top[..., None]), 0.0)
        factor = jnp.exp(top - new_top)
        total = total * factor + jnp.sum(probs, axis=-1)
        acc = acc * factor[..., None] + jnp.einsum(
            "hrk,hkd->hrd", probs, values.astype(jnp.float32)
        )
        return (new_top, total, acc)

    block = math.gcd(512, cache_len)
    blocks = cache_len // block
    cache_keys = kv_cache[0, 0].reshape(blocks, block, local_kv, DH).transpose(0, 2, 1, 3)
    cache_values = kv_cache[1, 0].reshape(blocks, block, local_kv, DH).transpose(0, 2, 1, 3)
    rows = group * span
    start_state = (
        jnp.full((local_kv, rows), NEGATIVE, jnp.float32),
        jnp.zeros((local_kv, rows), jnp.float32),
        jnp.zeros((local_kv, rows, DH), jnp.float32),
    )

    def cache_step(state, items):
        keys, values, index = items
        positions = shard_start + index * block + jnp.arange(block, dtype=jnp.int32)
        valid = jnp.broadcast_to((positions < prefix)[None, :], (rows, block))
        return (update(state, keys, values, valid), None)

    state, unused = lax.scan(
        cache_step, start_state, (cache_keys, cache_values, jnp.arange(blocks, dtype=jnp.int32))
    )
    block_keys = new_kv[0].reshape(span, local_kv, DH).transpose(1, 0, 2)
    block_values = new_kv[1].reshape(span, local_kv, DH).transpose(1, 0, 2)
    slots = jnp.arange(span, dtype=jnp.int32)[None, :]
    new_valid = (slots < length) & (slots <= row_pos[:, None]) & (width_index == 0)
    state = update(state, block_keys, block_values, new_valid)
    top, total, acc = merged(state, "ffn", combine_parts)
    heads = acc / total[..., None]
    attn = (
        heads.reshape(local_kv, group, span, DH)
        .transpose(2, 0, 1, 3)
        .reshape(span, qcols)
        .astype(jnp.bfloat16)
    )
    partial_value = jnp.dot(attn, out_weight, preferred_element_type=jnp.float32)
    summed = lax.psum(partial_value, "tp")
    h1 = (summed + resid.astype(jnp.float32)).astype(jnp.bfloat16)
    all_rows = lax.all_gather(h1, "grp", axis=0, tiled=True)
    rows_f = all_rows.astype(jnp.float32)
    squares = jnp.sum(rows_f * rows_f, axis=1)
    scaled = (rows_f * gain.astype(jnp.float32)[None, :]).astype(jnp.bfloat16)
    gate = jnp.dot(scaled, gate_weight, preferred_element_type=jnp.float32)
    upper = jnp.dot(scaled, up_weight, preferred_element_type=jnp.float32)
    rows_here = span // lax.axis_size("tp")
    gate, upper, squares = lax.psum((gate, upper, squares), "ffn")
    inv_rms = lax.rsqrt(squares / model + 1e-06)
    hidden = (jax.nn.silu(gate * inv_rms[:, None]) * (upper * inv_rms[:, None])).astype(
        jnp.bfloat16
    )
    down_rows = lax.psum_scatter(
        jnp.dot(hidden, down_weight, preferred_element_type=jnp.float32),
        ("grp", "tp"),
        scatter_dimension=0,
        tiled=True,
    )
    row_start = lax.axis_index("tp") * rows_here
    own = lax.dynamic_slice_in_dim(h1, row_start, rows_here, 0)
    live = row_start + jnp.arange(rows_here, dtype=jnp.int32) < length
    return jnp.where(live[:, None], own.astype(jnp.float32) + down_rows, 0.0).astype(jnp.bfloat16)


def solution(mesh):
    sizes = tuple(mesh.shape[axis] for axis in ("grp", "tp", "ffn"))
    return jax.shard_map(
        body if sizes == (2, 4, 4) else general_body,
        mesh=mesh,
        in_specs=(
            P("grp", "tp"),
            P(None, "grp", "tp"),
            P(None, "grp", "ffn", "tp"),
            P("grp"),
            P("grp"),
            P("grp", "ffn"),
            P("tp", "ffn"),
            P("ffn"),
            P("ffn", ("grp", "tp")),
            P("ffn", ("grp", "tp")),
            P(("grp", "tp"), "ffn"),
        ),
        out_specs=P(("grp", "tp"), "ffn"),
        check_vma=False,
    )
```

```python
import functools
import math

import jax
import jax.numpy as jnp
from jax import lax
from jax.experimental import pallas as pl
from jax.experimental.pallas import tpu as pltpu
from jax.sharding import PartitionSpec as P

DH = 128
TILE = 640
CHUNKS = (3, 3)
HEADS = 4
NEGATIVE = -1e30
BF16 = jnp.bfloat16
F32 = jnp.float32
LIMIT = 16 * 1024 * 1024
ORDER = (0, 2, 1, 3)


def swapped_bits(index):
    return (index & 1) * 2 + (index >> 1)


def params(limit=LIMIT):
    return pltpu.CompilerParams(vmem_limit_bytes=limit)


def cost(flops, moved, exps=0):
    return pl.CostEstimate(flops=int(flops), bytes_accessed=int(moved), transcendentals=int(exps))


def whole(shape):
    return pl.BlockSpec(shape, lambda *unused: (0,) * len(shape))


def fetch_kernel(source, target, zero, done):
    copy = pltpu.make_async_copy(source, target, done)
    copy.start()
    zero[...] = jnp.zeros_like(zero)
    copy.wait()


def fetch(weight, after):
    weight, after = lax.optimization_barrier((weight, after))
    weight = pltpu.with_memory_space_constraint(weight, pltpu.HBM)
    held, zero = pl.pallas_call(
        fetch_kernel,
        in_specs=[pl.BlockSpec(memory_space=pltpu.HBM)],
        out_specs=[pl.BlockSpec(memory_space=pltpu.VMEM)] * 2,
        out_shape=[
            jax.ShapeDtypeStruct(weight.shape, weight.dtype),
            jax.ShapeDtypeStruct((8, 128), F32),
        ],
        scratch_shapes=[pltpu.SemaphoreType.DMA],
        compiler_params=params(),
        cost_estimate=cost(0, 2 * weight.size * 2),
    )(weight)
    return held, zero, after


def attention_kernel(
    scalars, q_ref, key_ref, value_ref, new_key_ref, new_value_ref, sent_ref, kept_ref, sent_lse_ref, kept_lse_ref, columns
):
    step = pl.program_id(0)
    span = q_ref.shape[0]
    cache_len = key_ref.shape[2]
    per_kv = sent_lse_ref.shape[0]
    usable, length, first = scalars[1], scalars[2], scalars[3]
    scale = 1.0 / math.sqrt(DH)
    position = lax.broadcasted_iota(jnp.int32, (1, cache_len), 1)
    bias = jnp.where(position < usable, 0.0, NEGATIVE)
    row = lax.broadcasted_iota(jnp.int32, (span, span), 0)
    col = lax.broadcasted_iota(jnp.int32, (span, span), 1)
    allowed = (col <= row) & (col < length) & (first > 0)
    fresh_bias = jnp.concatenate([jnp.where(allowed, 0.0, NEGATIVE)] * HEADS, axis=0)
    contract = (((1,), (1,)), ((), ()))
    keys, values = key_ref[0, 0], value_ref[0, 0]
    new_keys, new_values = new_key_ref[0], new_value_ref[0]
    columns[...] = jnp.zeros_like(columns)
    for low in range(0, per_kv, HEADS):
        heads = range(low, low + HEADS)
        q = jnp.concatenate([q_ref[:, h * DH : (h + 1) * DH] for h in heads], axis=0)
        scores = lax.dot_general(q, keys, contract, preferred_element_type=F32) * scale + bias
        fresh = lax.dot_general(q, new_keys, contract, preferred_element_type=F32)
        fresh = fresh * scale + fresh_bias
        top = jnp.maximum(
            jnp.max(scores, axis=1, keepdims=True), jnp.max(fresh, axis=1, keepdims=True)
        )
        probs = jnp.exp(scores - top)
        fresh_probs = jnp.exp(fresh - top)
        total = jnp.sum(probs, axis=1, keepdims=True) + jnp.sum(fresh_probs, axis=1, keepdims=True)
        mixed = jnp.dot(probs.astype(BF16), values, preferred_element_type=F32)
        mixed += jnp.dot(fresh_probs.astype(BF16), new_values, preferred_element_type=F32)
        mixed = (mixed / total).astype(BF16)
        lse = top + jnp.log(total)
        for i, h in enumerate(heads):
            columns[0:span, h : h + 1] = lse[i * span : (i + 1) * span]
            piece = mixed[i * span : (i + 1) * span]

            @pl.when(step == 0)
            def to_sent():
                sent_ref[:, h * DH : (h + 1) * DH] = piece

            @pl.when(step == 1)
            def to_kept():
                kept_ref[:, h * DH : (h + 1) * DH] = piece

    rows = jnp.transpose(columns[...])[0:per_kv, :]

    @pl.when(step == 0)
    def lse_sent():
        sent_lse_ref[...] = rows

    @pl.when(step == 1)
    def lse_kept():
        kept_lse_ref[...] = rows


def attention(scalars, queries, kv_cache, new_kv):
    span, qcols = queries.shape
    per_kv = qcols // DH // 2
    cache_len = kv_cache.shape[2]
    width = per_kv * DH

    def which(i, s):
        return s[0] ^ 1 ^ i

    def at_home(array):
        return pltpu.with_memory_space_constraint(array, pltpu.HBM)

    call = pl.pallas_call(
        attention_kernel,
        grid_spec=pltpu.PrefetchScalarGridSpec(
            num_scalar_prefetch=1,
            grid=(2,),
            in_specs=[
                pl.BlockSpec((span, width), lambda i, s: (0, which(i, s))),
                pl.BlockSpec((1, 1, cache_len, DH), lambda i, s: (0, 0, 0, which(i, s))),
                pl.BlockSpec((1, 1, cache_len, DH), lambda i, s: (1, 0, 0, which(i, s))),
                pl.BlockSpec((1, span, DH), lambda i, s: (0, 0, which(i, s))),
                pl.BlockSpec((1, span, DH), lambda i, s: (1, 0, which(i, s))),
            ],
            out_specs=[whole((span, width))] * 2 + [whole((per_kv, 128))] * 2,
            scratch_shapes=[pltpu.VMEM((128, 128), F32)],
        ),
        out_shape=[jax.ShapeDtypeStruct((span, width), BF16)] * 2
        + [jax.ShapeDtypeStruct((per_kv, 128), F32)] * 2,
        compiler_params=params(40 * 1024 * 1024),
        cost_estimate=cost(
            8 * span * per_kv * cache_len * DH, 8 * cache_len * DH, 2 * span * per_kv * cache_len
        ),
    )
    queries, kv_cache, new_kv = at_home(queries), at_home(kv_cache), at_home(new_kv)
    return call(scalars, queries, kv_cache, kv_cache, new_kv, new_kv)


def combine_kernel(a_ref, b_ref, lse_a_ref, lse_b_ref, out_ref, lse_ref):
    span = a_ref.shape[0]
    heads = lse_a_ref.shape[0]
    lse_a, lse_b = lse_a_ref[...], lse_b_ref[...]
    top = jnp.maximum(lse_a, lse_b)
    left, right = jnp.exp(lse_a - top), jnp.exp(lse_b - top)
    total = left + right
    lse_ref[...] = top + jnp.log(total)
    rest = jnp.zeros((128 - 2 * heads, 128), F32)
    table = jnp.transpose(jnp.concatenate([left / total, right / total, rest], axis=0))
    for h in range(heads):
        cols = slice(h * DH, (h + 1) * DH)
        mixed = a_ref[:, cols].astype(F32) * table[0:span, h : h + 1]
        mixed += b_ref[:, cols].astype(F32) * table[0:span, heads + h : heads + h + 1]
        out_ref[:, cols] = mixed.astype(BF16)


def combine(a, b, lse_a, lse_b):
    return pl.pallas_call(
        combine_kernel,
        out_shape=[
            jax.ShapeDtypeStruct(a.shape, BF16),
            jax.ShapeDtypeStruct(lse_a.shape, F32),
        ],
        compiler_params=params(),
        cost_estimate=cost(4 * a.size, 6 * a.size),
    )(a, b, lse_a, lse_b)


def project_kernel(scalars, keep_ref, other_ref, weight_ref, *rest):
    outs, acc = rest[:-1], rest[-1]
    step = pl.program_id(0)
    depth = weight_ref.shape[0]
    half = pl.num_programs(0) // 2
    rows = outs[0].shape[0]

    @pl.when(step < half)
    def from_keep():
        start = pl.multiple_of(step * depth, depth)
        term = jnp.dot(keep_ref[:, pl.ds(start, depth)], weight_ref[...], preferred_element_type=F32)

        @pl.when(step == 0)
        def begin():
            acc[...] = term

        @pl.when(step > 0)
        def go_on():
            acc[...] += term

    @pl.when(step >= half)
    def from_other():
        start = pl.multiple_of((step - half) * depth, depth)
        acc[...] += jnp.dot(
            other_ref[:, pl.ds(start, depth)], weight_ref[...], preferred_element_type=F32
        )

    @pl.when(step == pl.num_programs(0) - 1)
    def finish():
        for k, out in enumerate(outs):
            start = pl.multiple_of((scalars[4] ^ k) * rows, 8)
            out[...] = acc[pl.ds(start, rows), :].astype(out.dtype)


def project(scalars, keep, other, out_weight, tp_size):
    span, width = keep.shape
    depth = 512
    half = width // depth
    cols = out_weight.shape[1]
    rows = span // tp_size
    return pl.pallas_call(
        project_kernel,
        grid_spec=pltpu.PrefetchScalarGridSpec(
            num_scalar_prefetch=1,
            grid=(2 * half,),
            in_specs=[
                whole((span, width)),
                whole((span, width)),
                pl.BlockSpec(
                    (depth, cols),
                    lambda i, s: (jnp.where(i < half, s[0], 1 - s[0]) * half + i % half, 0),
                ),
            ],
            out_specs=[whole((rows, cols))] * tp_size,
            scratch_shapes=[pltpu.VMEM((span, cols), F32)],
        ),
        out_shape=[
            jax.ShapeDtypeStruct((rows, cols), F32 if k == 0 else BF16) for k in range(tp_size)
        ],
        compiler_params=params(),
        cost_estimate=cost(4 * span * width * cols, 4 * width * cols),
    )(scalars, keep, other, out_weight)


def scale_kernel(slots, scalars, *refs):
    count = 4 * slots
    sources, gain_ref, scaled_ref, square_ref, ordered = refs[:count], *refs[count:]
    gain = gain_ref[...].astype(F32)
    cols = gain.shape[1]
    for k in range(4):
        place = swapped_bits(scalars[5] ^ k)
        rows = jnp.concatenate(
            [sources[k * slots + s][...].astype(F32) for s in range(slots)], axis=0
        )
        ordered[place] = rows * gain
        squares = rows * rows
        part = squares[:, 0:128]
        for c in range(128, cols, 128):
            part += squares[:, c : c + 128]
        square_ref[place] = part
    tall = ordered[...].reshape(scaled_ref.shape[1], cols)
    scaled_ref[...] = jnp.transpose(tall).astype(BF16)


def scale_rows(scalars, sources, gain):
    slots = len(sources) // 4
    rows, cols = sources[0].shape
    high = rows * slots
    return pl.pallas_call(
        functools.partial(scale_kernel, slots),
        grid_spec=pltpu.PrefetchScalarGridSpec(
            num_scalar_prefetch=1,
            grid=(1,),
            in_specs=[whole((rows, cols))] * len(sources) + [whole((1, cols))],
            out_specs=[whole((cols, 4 * high)), whole((4, high, 128))],
            scratch_shapes=[pltpu.VMEM((4, high, cols), F32)],
        ),
        out_shape=[
            jax.ShapeDtypeStruct((cols, 4 * high), BF16),
            jax.ShapeDtypeStruct((4, high, 128), F32),
        ],
        compiler_params=params(),
        cost_estimate=cost(4 * 4 * high * cols, 4 * 4 * high * cols),
    )(scalars, *sources, gain)


def gate_up_kernel(scaled_ref, gate_ref, up_ref, keep_ref, cross_ref, send_ref):
    high = keep_ref.shape[1]
    for which, weight in enumerate((gate_ref, up_ref)):
        term = jnp.dot(weight[...], scaled_ref[...], preferred_element_type=F32)
        term = jnp.transpose(term).astype(BF16)
        keep_ref[which] = term[0:high]
        cross_ref[which] = term[high : 2 * high]
        send_ref[0, which] = term[2 * high : 3 * high]
        send_ref[1, which] = term[3 * high :]


def gate_up(scaled, gate_weight, up_weight, begin, width):
    depth, rows = scaled.shape
    high = rows // 4
    tiles = pl.cdiv(width, TILE)
    first = begin // TILE
    weight = pl.BlockSpec((TILE, depth), lambda j: (first + j, 0))
    piece = pl.BlockSpec((2, high, TILE), lambda j: (0, 0, j))
    return pl.pallas_call(
        gate_up_kernel,
        grid=(tiles,),
        in_specs=[whole(scaled.shape), weight, weight],
        out_specs=[piece, piece, pl.BlockSpec((2, 2, high, TILE), lambda j: (0, 0, 0, j))],
        out_shape=[
            jax.ShapeDtypeStruct((2, high, width), BF16),
            jax.ShapeDtypeStruct((2, high, width), BF16),
            jax.ShapeDtypeStruct((2, 2, high, width), BF16),
        ],
        compiler_params=params(),
        cost_estimate=cost(4 * rows * depth * width, 4 * depth * width),
    )(scaled, gate_weight, up_weight)


def down_kernel(width, slots, has_start, last, scalars, *refs):
    hidden = refs[0:4]
    weight_ref = refs[4]
    rest = list(refs[5:])
    start_ref = rest.pop(0) if has_start else None
    acc, packed = rest[-2], rest[-1]
    outs = rest[:-2]
    step = pl.program_id(0)
    depth = weight_ref.shape[0]
    high = hidden[0].shape[0]
    steps = pl.num_programs(0)

    @pl.when(step == 0)
    def begin():
        if width % depth:
            packed[...] = jnp.zeros_like(packed)
        for place in range(4):
            packed[place * high : (place + 1) * high, 0:width] = hidden[place][...]
        if has_start:
            acc[...] = start_ref[...]
        else:
            acc[...] = jnp.zeros_like(acc)

    start = pl.multiple_of(step * depth, depth)

    def add(weight):
        term = jnp.dot(packed[:, pl.ds(start, depth)], weight, preferred_element_type=F32)
        acc[...] += term.reshape(acc.shape)

    if width % depth:

        @pl.when(step < steps - 1)
        def inner():
            add(weight_ref[...])

        @pl.when(step == steps - 1)
        def edge():
            row = lax.broadcasted_iota(jnp.int32, weight_ref.shape, 0)
            add(jnp.where(row < width % depth, weight_ref[...], jnp.zeros_like(weight_ref)))
    else:
        add(weight_ref[...])

    @pl.when(step == steps - 1)
    def finish():
        if not last:
            outs[0][...] = acc[...]
            return
        rows = high // slots
        for k in range(4):
            place = swapped_bits(scalars[5] ^ k)
            block = acc[place]
            for s in range(slots):
                out = outs[k * slots + s]
                out[...] = block[s * rows : (s + 1) * rows].astype(out.dtype)


def down(scalars, hidden, down_weight, begin, start, slots, last):
    high, width = hidden[0].shape
    cols = down_weight.shape[1]
    steps = pl.cdiv(width, TILE)
    first = begin // TILE
    rows = high // slots
    ins = [whole((high, width))] * 4 + [pl.BlockSpec((TILE, cols), lambda i, s: (first + i, 0))]
    args = list(hidden) + [down_weight]
    if start is not None:
        ins.append(whole((4, high, cols)))
        args.append(start)
    if last:
        shapes = [
            jax.ShapeDtypeStruct((rows, cols), F32 if s == 0 else BF16)
            for k in range(4)
            for s in range(slots)
        ]
    else:
        shapes = [jax.ShapeDtypeStruct((4, high, cols), F32)]
    return pl.pallas_call(
        functools.partial(down_kernel, width, slots, start is not None, last),
        grid_spec=pltpu.PrefetchScalarGridSpec(
            num_scalar_prefetch=1,
            grid=(steps,),
            in_specs=ins,
            out_specs=[whole(shape.shape) for shape in shapes],
            scratch_shapes=[
                pltpu.VMEM((4, high, cols), F32),
                pltpu.VMEM((4 * high, steps * TILE), BF16),
            ],
        ),
        out_shape=shapes,
        compiler_params=params(),
        cost_estimate=cost(8 * high * width * cols, 2 * width * cols),
    )(scalars, *args)


def to_core(x):
    return lax.ppermute(x, "ffn", [(i, i ^ 1) for i in range(4)])


def to_x(x):
    return lax.ppermute(x, "ffn", [(i, i ^ 2) for i in range(4)])


def to_z(x, k):
    return lax.ppermute(x, "tp", [(i, i ^ k) for i in range(4)])


def to_y(x):
    return lax.ppermute(x, "grp", [(0, 1), (1, 0)])


def cut(total):
    edges = [0]
    for tiles in CHUNKS:
        edges.append(min(edges[-1] + tiles * TILE, total))
    return [(low, high - low) for low, high in zip(edges, edges[1:])]


def body(
    queries,
    new_kv,
    kv_cache,
    lengths,
    prefixes,
    resid,
    out_weight,
    gain,
    gate_weight,
    up_weight,
    down_weight,
):
    span = queries.shape[0]
    local_kv = new_kv.shape[2] // DH
    cache_len = kv_cache.shape[2]
    groups = lax.axis_size("grp")
    tp_size = lax.axis_size("tp")
    g, t, f = lax.axis_index("grp"), lax.axis_index("tp"), lax.axis_index("ffn")
    core = f & 1
    length = lengths[0]
    rows = span // tp_size
    model = gain.shape[0] * lax.axis_size("ffn")
    usable = jnp.clip(prefixes[0] - f * cache_len, 0, cache_len)
    first = (f == 0).astype(jnp.int32)
    scalars = jnp.stack([core, usable, length, first, t, t ^ f]).astype(jnp.int32)
    own_resid = lax.dynamic_slice_in_dim(resid, t * rows, rows, 0).astype(F32)
    live = (t * rows + jnp.arange(rows, dtype=jnp.int32) < length)[:, None]
    live = jnp.broadcast_to(live, (rows, 128)).astype(F32)
    scalars, own_resid, live = lax.optimization_barrier((scalars, own_resid, live))
    sent, kept, sent_lse, kept_lse = attention(scalars, queries, kv_cache, new_kv)
    got, got_lse = to_core(sent), to_core(sent_lse)
    kept, kept_lse = combine(kept, got, kept_lse, got_lse)
    out_held, zero, kept = fetch(out_weight, kept)
    got, got_lse = to_x(kept), to_x(kept_lse) + zero
    mine, unused = combine(kept, got, kept_lse, got_lse)
    other = to_core(mine)

    terms = list(project(scalars, mine, other, out_held, tp_size))
    gate_held, zero, terms[1] = fetch(gate_weight.T, terms[1])
    passed = [to_z(terms[k], k) for k in (1, 3, 2)]
    summed = terms[0] + own_resid + zero[0:1, 0:1]
    for term in passed:
        summed += term.astype(F32)
    h1 = summed.astype(BF16)

    natural = g ^ jnp.arange(groups, dtype=jnp.int32)
    by_z = [h1, to_z(h1, 1), to_z(h1, 2), to_z(h1, 3)]
    up_held, unused, by_z[1] = fetch(up_weight.T, by_z[1])
    sources = []
    for part in by_z:
        if groups == 2:
            sources += [part, to_y(part)]
        else:
            everyone = jnp.take(lax.all_gather(part, "grp"), natural, axis=0)
            sources += [everyone[s] for s in range(groups)]
    scaled, squares = scale_rows(scalars, sources, gain[None, :])

    chunks = cut(gate_weight.shape[1])
    reduced = []
    for begin, width in chunks:
        keep, cross, send = gate_up(scaled, gate_held, up_held, begin, width)
        got = to_core(send)
        cross = (cross.astype(F32) + got[1].astype(F32)).astype(BF16)
        scaled, cross = lax.optimization_barrier((scaled, cross))
        reduced.append((keep, got, to_x(cross)))
        if begin == 0:
            squares, scaled = lax.optimization_barrier((squares, scaled))
            pair = squares[0:2] + to_core(squares[2:4])
            own_squares = pair[0] + to_x(pair[1])
    inv_rms = lax.rsqrt(jnp.sum(own_squares, axis=1, keepdims=True) / model + 1e-06)
    total = None
    for index, (begin, width) in enumerate(chunks):
        keep, got, crossed = reduced[index]
        both = (keep.astype(F32) + got[0].astype(F32) + crossed.astype(F32)) * inv_rms
        hidden = (jax.nn.silu(both[0]) * both[1]).astype(BF16)
        if index == 0:
            down_held, zero, hidden = fetch(down_weight, hidden)
            inv_rms += zero[0:1, 0:1]
        over = to_x(hidden)
        if index > 0:
            over, total = lax.optimization_barrier((over, total))
        pieces = [hidden, over, to_core(hidden), to_core(over)]
        is_last = index == len(chunks) - 1
        result = down(scalars, pieces, down_held, begin, total, groups, is_last)
        total = None if is_last else result[0]

    chunk_sums = []
    for k in range(4):
        own = result[k * groups]
        others = result[k * groups + 1 : (k + 1) * groups]
        if groups == 2:
            chunk_sums.append((own, others[0]))
        else:
            stacked = jnp.stack([own.astype(BF16)] + list(others))
            stacked = jnp.take(stacked, natural, axis=0)
            moved = lax.all_to_all(stacked, "grp", split_axis=0, concat_axis=0, tiled=True)
            chunk_sums.append(jnp.sum(moved.astype(F32), axis=0))
    out = h1.astype(F32)
    for k in (3, 2, 1, 0):
        if groups == 2:
            own, away = chunk_sums[k]
            value = own + to_y(away).astype(F32)
        else:
            value = chunk_sums[k]
        out += value if k == 0 else to_z(value.astype(BF16), k).astype(F32)
    return jnp.where(live[:, 0:1] > 0, out, 0.0).astype(BF16)


def merged(x, axis, combine):
    everything = jax.tree.map(lambda part: lax.all_gather(part, axis), x)
    leading = jax.tree.map(lambda part: part[0], everything)

    def hop(k, so_far):
        return combine(so_far, jax.tree.map(lambda part: part[k], everything))

    return lax.fori_loop(1, lax.axis_size(axis), hop, leading)


def combine_parts(first, second):
    top = jnp.maximum(first[0], second[0])
    left = jnp.exp(first[0] - top)
    right = jnp.exp(second[0] - top)
    total = first[1] * left + second[1] * right
    values = first[2] * left[..., None] + second[2] * right[..., None]
    return (top, total, values)


def general_body(
    queries,
    new_kv,
    kv_cache,
    lengths,
    prefixes,
    resid,
    out_weight,
    gain,
    gate_weight,
    up_weight,
    down_weight,
):
    span, qcols = queries.shape
    kcols = new_kv.shape[2]
    local_kv = kcols // DH
    group = qcols // DH // local_kv
    cache_len = kv_cache.shape[2]
    length = lengths[0]
    model = gain.shape[0] * lax.axis_size("ffn")
    prefix = prefixes[0]
    width_index = lax.axis_index("ffn")
    shard_start = width_index * cache_len
    query_heads = (
        queries.reshape(span, local_kv, group, DH)
        .transpose(1, 2, 0, 3)
        .reshape(local_kv, group * span, DH)
    )
    row_pos = jnp.tile(jnp.arange(span, dtype=jnp.int32), group)
    inv_scale = 1.0 / math.sqrt(DH)

    def update(state, keys, values, valid):
        top, total, acc = state
        scores = (
            jnp.einsum("hrd,hkd->hrk", query_heads, keys, preferred_element_type=jnp.float32)
            * inv_scale
        )
        scores = jnp.where(valid[None], scores, NEGATIVE)
        new_top = jnp.maximum(top, jnp.max(scores, axis=-1))
        probs = jnp.where(valid[None], jnp.exp(scores - new_top[..., None]), 0.0)
        factor = jnp.exp(top - new_top)
        total = total * factor + jnp.sum(probs, axis=-1)
        acc = acc * factor[..., None] + jnp.einsum(
            "hrk,hkd->hrd", probs, values.astype(jnp.float32)
        )
        return (new_top, total, acc)

    block = math.gcd(512, cache_len)
    blocks = cache_len // block
    cache_keys = kv_cache[0, 0].reshape(blocks, block, local_kv, DH).transpose(0, 2, 1, 3)
    cache_values = kv_cache[1, 0].reshape(blocks, block, local_kv, DH).transpose(0, 2, 1, 3)
    rows = group * span
    start_state = (
        jnp.full((local_kv, rows), NEGATIVE, jnp.float32),
        jnp.zeros((local_kv, rows), jnp.float32),
        jnp.zeros((local_kv, rows, DH), jnp.float32),
    )

    def cache_step(state, items):
        keys, values, index = items
        positions = shard_start + index * block + jnp.arange(block, dtype=jnp.int32)
        valid = jnp.broadcast_to((positions < prefix)[None, :], (rows, block))
        return (update(state, keys, values, valid), None)

    state, unused = lax.scan(
        cache_step, start_state, (cache_keys, cache_values, jnp.arange(blocks, dtype=jnp.int32))
    )
    block_keys = new_kv[0].reshape(span, local_kv, DH).transpose(1, 0, 2)
    block_values = new_kv[1].reshape(span, local_kv, DH).transpose(1, 0, 2)
    slots = jnp.arange(span, dtype=jnp.int32)[None, :]
    new_valid = (slots < length) & (slots <= row_pos[:, None]) & (width_index == 0)
    state = update(state, block_keys, block_values, new_valid)
    top, total, acc = merged(state, "ffn", combine_parts)
    heads = acc / total[..., None]
    attn = (
        heads.reshape(local_kv, group, span, DH)
        .transpose(2, 0, 1, 3)
        .reshape(span, qcols)
        .astype(jnp.bfloat16)
    )
    partial_value = jnp.dot(attn, out_weight, preferred_element_type=jnp.float32)
    summed = lax.psum(partial_value, "tp")
    h1 = (summed + resid.astype(jnp.float32)).astype(jnp.bfloat16)
    all_rows = lax.all_gather(h1, "grp", axis=0, tiled=True)
    rows_f = all_rows.astype(jnp.float32)
    squares = jnp.sum(rows_f * rows_f, axis=1)
    scaled = (rows_f * gain.astype(jnp.float32)[None, :]).astype(jnp.bfloat16)
    gate = jnp.dot(scaled, gate_weight, preferred_element_type=jnp.float32)
    upper = jnp.dot(scaled, up_weight, preferred_element_type=jnp.float32)
    rows_here = span // lax.axis_size("tp")
    gate, upper, squares = lax.psum((gate, upper, squares), "ffn")
    inv_rms = lax.rsqrt(squares / model + 1e-06)
    hidden = (jax.nn.silu(gate * inv_rms[:, None]) * (upper * inv_rms[:, None])).astype(
        jnp.bfloat16
    )
    down_rows = lax.psum_scatter(
        jnp.dot(hidden, down_weight, preferred_element_type=jnp.float32),
        ("grp", "tp"),
        scatter_dimension=0,
        tiled=True,
    )
    row_start = lax.axis_index("tp") * rows_here
    own = lax.dynamic_slice_in_dim(h1, row_start, rows_here, 0)
    live = row_start + jnp.arange(rows_here, dtype=jnp.int32) < length
    return jnp.where(live[:, None], own.astype(jnp.float32) + down_rows, 0.0).astype(jnp.bfloat16)


def solution(mesh):
    sizes = tuple(mesh.shape[axis] for axis in ("grp", "tp", "ffn"))
    return jax.shard_map(
        body if sizes == (2, 4, 4) else general_body,
        mesh=mesh,
        in_specs=(
            P("grp", "tp"),
            P(None, "grp", "tp"),
            P(None, "grp", "ffn", "tp"),
            P("grp"),
            P("grp"),
            P("grp", "ffn"),
            P("tp", "ffn"),
            P("ffn"),
            P("ffn", ("grp", "tp")),
            P("ffn", ("grp", "tp")),
            P(("grp", "tp"), "ffn"),
        ),
        out_specs=P(("grp", "tp"), "ffn"),
        check_vma=False,
    )
```

```python
import functools
import math

import jax
import jax.numpy as jnp
from jax import lax
from jax.experimental import pallas as pl
from jax.experimental.pallas import tpu as pltpu
from jax.sharding import PartitionSpec as P

DH = 128
TILE = 640
CHUNKS = (3, 3)
HEADS = 4
THIN = 1
NEGATIVE = -1e30
BF16 = jnp.bfloat16
F32 = jnp.float32
LIMIT = 8 * 1024 * 1024
ORDER = (0, 2, 1, 3)


def swapped_bits(index):
    return (index & 1) * 2 + (index >> 1)


def params(limit=LIMIT):
    return pltpu.CompilerParams(vmem_limit_bytes=limit)


def cost(flops, moved, exps=0):
    return pl.CostEstimate(
        flops=int(flops) // THIN, bytes_accessed=int(moved) // THIN, transcendentals=int(exps) // THIN
    )


def whole(shape):
    return pl.BlockSpec(shape, lambda *unused: (0,) * len(shape))


def fetch_kernel(pieces, *refs):
    count = len(pieces)
    sources, targets, mark, done = refs[:count], refs[count : 2 * count], refs[-2], refs[-1]
    copies = []
    for i, (begin, width) in enumerate(pieces):
        source = sources[i].at[pl.ds(begin, width)]
        copies.append(pltpu.make_async_copy(source, targets[i], done.at[i]))
    for copy in copies:
        copy.start()
    mark[...] = jnp.zeros_like(mark)
    for copy in copies:
        copy.wait()


def fetch(weights, pieces, after):
    *weights, after = lax.optimization_barrier((*weights, after))
    weights = [pltpu.with_memory_space_constraint(weight, pltpu.HBM) for weight in weights]
    shapes = [
        jax.ShapeDtypeStruct((width, weight.shape[1]), weight.dtype)
        for weight, (begin, width) in zip(weights, pieces)
    ]
    *held, mark = pl.pallas_call(
        functools.partial(fetch_kernel, pieces),
        in_specs=[pl.BlockSpec(memory_space=pltpu.HBM)] * len(weights),
        out_specs=[pl.BlockSpec(memory_space=pltpu.VMEM)] * (len(weights) + 1),
        out_shape=shapes + [jax.ShapeDtypeStruct((8, 128), F32)],
        scratch_shapes=[pltpu.SemaphoreType.DMA((len(weights),))],
        compiler_params=params(),
        cost_estimate=cost(0, 4 * sum(shape.size for shape in shapes)),
    )(*weights)
    return held, mark, after


def attention_kernel(
    scalars, q_ref, key_ref, value_ref, new_key_ref, new_value_ref, sent_ref, kept_ref, sent_lse_ref, kept_lse_ref, columns
):
    step = pl.program_id(0)
    span = q_ref.shape[0]
    cache_len = key_ref.shape[2]
    per_kv = sent_lse_ref.shape[0]
    usable, length, first = scalars[1], scalars[2], scalars[3]
    scale = 1.0 / math.sqrt(DH)
    position = lax.broadcasted_iota(jnp.int32, (1, cache_len), 1)
    bias = jnp.where(position < usable, 0.0, NEGATIVE)
    row = lax.broadcasted_iota(jnp.int32, (span, span), 0)
    col = lax.broadcasted_iota(jnp.int32, (span, span), 1)
    allowed = (col <= row) & (col < length) & (first > 0)
    fresh_bias = jnp.concatenate([jnp.where(allowed, 0.0, NEGATIVE)] * HEADS, axis=0)
    contract = (((1,), (1,)), ((), ()))
    keys, values = key_ref[0, 0], value_ref[0, 0]
    new_keys, new_values = new_key_ref[0], new_value_ref[0]
    columns[...] = jnp.zeros_like(columns)
    for low in range(0, per_kv, HEADS):
        heads = range(low, low + HEADS)
        q = jnp.concatenate([q_ref[:, h * DH : (h + 1) * DH] for h in heads], axis=0)
        scores = lax.dot_general(q, keys, contract, preferred_element_type=F32) * scale + bias
        fresh = lax.dot_general(q, new_keys, contract, preferred_element_type=F32)
        fresh = fresh * scale + fresh_bias
        top = jnp.maximum(
            jnp.max(scores, axis=1, keepdims=True), jnp.max(fresh, axis=1, keepdims=True)
        )
        probs = jnp.exp(scores - top)
        fresh_probs = jnp.exp(fresh - top)
        total = jnp.sum(probs, axis=1, keepdims=True) + jnp.sum(fresh_probs, axis=1, keepdims=True)
        mixed = jnp.dot(probs.astype(BF16), values, preferred_element_type=F32)
        mixed += jnp.dot(fresh_probs.astype(BF16), new_values, preferred_element_type=F32)
        mixed = (mixed / total).astype(BF16)
        lse = top + jnp.log(total)
        for i, h in enumerate(heads):
            columns[0:span, h : h + 1] = lse[i * span : (i + 1) * span]
            piece = mixed[i * span : (i + 1) * span]

            @pl.when(step == 0)
            def to_sent():
                sent_ref[:, h * DH : (h + 1) * DH] = piece

            @pl.when(step == 1)
            def to_kept():
                kept_ref[:, h * DH : (h + 1) * DH] = piece

    rows = jnp.transpose(columns[...])[0:per_kv, :]

    @pl.when(step == 0)
    def lse_sent():
        sent_lse_ref[...] = rows

    @pl.when(step == 1)
    def lse_kept():
        kept_lse_ref[...] = rows


def attention(scalars, queries, kv_cache, new_kv):
    span, qcols = queries.shape
    per_kv = qcols // DH // 2
    cache_len = kv_cache.shape[2]
    width = per_kv * DH

    def which(i, s):
        return s[0] ^ 1 ^ i

    def at_home(array):
        return pltpu.with_memory_space_constraint(array, pltpu.HBM)

    call = pl.pallas_call(
        attention_kernel,
        grid_spec=pltpu.PrefetchScalarGridSpec(
            num_scalar_prefetch=1,
            grid=(2,),
            in_specs=[
                pl.BlockSpec((span, width), lambda i, s: (0, which(i, s))),
                pl.BlockSpec((1, 1, cache_len, DH), lambda i, s: (0, 0, 0, which(i, s))),
                pl.BlockSpec((1, 1, cache_len, DH), lambda i, s: (1, 0, 0, which(i, s))),
                pl.BlockSpec((1, span, DH), lambda i, s: (0, 0, which(i, s))),
                pl.BlockSpec((1, span, DH), lambda i, s: (1, 0, which(i, s))),
            ],
            out_specs=[whole((span, width))] * 2 + [whole((per_kv, 128))] * 2,
            scratch_shapes=[pltpu.VMEM((128, 128), F32)],
        ),
        out_shape=[jax.ShapeDtypeStruct((span, width), BF16)] * 2
        + [jax.ShapeDtypeStruct((per_kv, 128), F32)] * 2,
        compiler_params=params(40 * 1024 * 1024),
        cost_estimate=cost(
            8 * span * per_kv * cache_len * DH, 8 * cache_len * DH, 2 * span * per_kv * cache_len
        ),
    )
    queries, kv_cache, new_kv = at_home(queries), at_home(kv_cache), at_home(new_kv)
    return call(scalars, queries, kv_cache, kv_cache, new_kv, new_kv)


def combine_kernel(a_ref, b_ref, lse_a_ref, lse_b_ref, *rest):
    out_ref, lse_ref = rest[-2:]
    span = a_ref.shape[0]
    heads = lse_a_ref.shape[0]
    lse_a, lse_b = lse_a_ref[...], lse_b_ref[...]
    top = jnp.maximum(lse_a, lse_b)
    left, right = jnp.exp(lse_a - top), jnp.exp(lse_b - top)
    total = left + right
    lse_ref[...] = top + jnp.log(total)
    rest = jnp.zeros((128 - 2 * heads, 128), F32)
    table = jnp.transpose(jnp.concatenate([left / total, right / total, rest], axis=0))
    for h in range(heads):
        cols = slice(h * DH, (h + 1) * DH)
        mixed = a_ref[:, cols].astype(F32) * table[0:span, h : h + 1]
        mixed += b_ref[:, cols].astype(F32) * table[0:span, heads + h : heads + h + 1]
        out_ref[:, cols] = mixed.astype(BF16)


def combine(a, b, lse_a, lse_b, *behind):
    return pl.pallas_call(
        combine_kernel,
        out_shape=[
            jax.ShapeDtypeStruct(a.shape, BF16),
            jax.ShapeDtypeStruct(lse_a.shape, F32),
        ],
        compiler_params=params(),
        cost_estimate=cost(4 * a.size, 6 * a.size),
    )(a, b, lse_a, lse_b, *behind)


def project_kernel(scalars, keep_ref, other_ref, weight_ref, *rest):
    outs, acc = rest[:-1], rest[-1]
    step = pl.program_id(0)
    depth = weight_ref.shape[0]
    half = pl.num_programs(0) // 2
    rows = outs[0].shape[0]

    @pl.when(step < half)
    def from_keep():
        start = pl.multiple_of(step * depth, depth)
        term = jnp.dot(keep_ref[:, pl.ds(start, depth)], weight_ref[...], preferred_element_type=F32)

        @pl.when(step == 0)
        def begin():
            acc[...] = term

        @pl.when(step > 0)
        def go_on():
            acc[...] += term

    @pl.when(step >= half)
    def from_other():
        start = pl.multiple_of((step - half) * depth, depth)
        acc[...] += jnp.dot(
            other_ref[:, pl.ds(start, depth)], weight_ref[...], preferred_element_type=F32
        )

    @pl.when(step == pl.num_programs(0) - 1)
    def finish():
        for k, out in enumerate(outs):
            start = pl.multiple_of((scalars[4] ^ k) * rows, 8)
            out[...] = acc[pl.ds(start, rows), :].astype(out.dtype)


def project(scalars, keep, other, out_weight, tp_size):
    span, width = keep.shape
    depth = 512
    half = width // depth
    cols = out_weight.shape[1]
    rows = span // tp_size
    return pl.pallas_call(
        project_kernel,
        grid_spec=pltpu.PrefetchScalarGridSpec(
            num_scalar_prefetch=1,
            grid=(2 * half,),
            in_specs=[
                whole((span, width)),
                whole((span, width)),
                pl.BlockSpec(
                    (depth, cols),
                    lambda i, s: (jnp.where(i < half, s[0], 1 - s[0]) * half + i % half, 0),
                ),
            ],
            out_specs=[whole((rows, cols))] * tp_size,
            scratch_shapes=[pltpu.VMEM((span, cols), F32)],
        ),
        out_shape=[
            jax.ShapeDtypeStruct((rows, cols), F32 if k == 0 else BF16) for k in range(tp_size)
        ],
        compiler_params=params(),
        cost_estimate=cost(4 * span * width * cols, 4 * width * cols),
    )(scalars, keep, other, out_weight)


def residual_kernel(scalars, resid_ref, first_ref, *rest):
    out_ref, spread = rest[-2:]
    rows = out_ref.shape[0]
    spread[...] = resid_ref[...].astype(F32)
    total = first_ref[...] + spread[pl.ds(pl.multiple_of(scalars[4] * rows, 8), rows), :]
    for term in rest[:3]:
        total += term[...].astype(F32)
    out_ref[...] = total.astype(BF16)


def add_residual(scalars, resid, first, others, *behind):
    shape = first.shape
    ins = [resid, first, *others, *behind]
    return pl.pallas_call(
        residual_kernel,
        grid_spec=pltpu.PrefetchScalarGridSpec(
            num_scalar_prefetch=1,
            grid=(1,),
            in_specs=[whole(part.shape) for part in ins],
            out_specs=whole(shape),
            scratch_shapes=[pltpu.VMEM(resid.shape, F32)],
        ),
        out_shape=jax.ShapeDtypeStruct(shape, BF16),
        compiler_params=params(),
        cost_estimate=cost(5 * first.size, 12 * first.size),
    )(scalars, *ins)


def scale_kernel(slots, scalars, *refs):
    count = 4 * slots
    sources, gain_ref = refs[:count], refs[count]
    scaled_ref, square_ref, ordered = refs[-3:]
    gain = gain_ref[...].astype(F32)
    cols = gain.shape[1]
    for k in range(4):
        place = swapped_bits(scalars[5] ^ k)
        rows = jnp.concatenate(
            [sources[k * slots + s][...].astype(F32) for s in range(slots)], axis=0
        )
        ordered[place] = rows * gain
        squares = rows * rows
        part = squares[:, 0:128]
        for c in range(128, cols, 128):
            part += squares[:, c : c + 128]
        square_ref[place] = part
    tall = ordered[...].reshape(scaled_ref.shape[1], cols)
    scaled_ref[...] = jnp.transpose(tall).astype(BF16)


def scale_rows(scalars, sources, gain, mark):
    slots = len(sources) // 4
    rows, cols = sources[0].shape
    high = rows * slots
    return pl.pallas_call(
        functools.partial(scale_kernel, slots),
        grid_spec=pltpu.PrefetchScalarGridSpec(
            num_scalar_prefetch=1,
            grid=(1,),
            in_specs=[whole((rows, cols))] * len(sources) + [whole((1, cols)), whole(mark.shape)],
            out_specs=[whole((cols, 4 * high)), whole((4, high, 128))],
            scratch_shapes=[pltpu.VMEM((4, high, cols), F32)],
        ),
        out_shape=[
            jax.ShapeDtypeStruct((cols, 4 * high), BF16),
            jax.ShapeDtypeStruct((4, high, 128), F32),
        ],
        compiler_params=params(),
        cost_estimate=cost(4 * 4 * high * cols, 4 * 4 * high * cols),
    )(scalars, *sources, gain, mark)


def gate_up_kernel(tiles, scaled_ref, gate_ref, up_ref, *rest):
    keep_ref, cross_ref, send_ref = rest[-3:]
    high = keep_ref.shape[1]
    homes = (keep_ref, cross_ref, send_ref.at[0], send_ref.at[1])

    def multiply():
        for which, weight in enumerate((gate_ref, up_ref)):
            term = jnp.dot(weight[...], scaled_ref[...], preferred_element_type=F32)
            term = jnp.transpose(term).astype(BF16)
            for place, home in enumerate(homes):
                home[which] = term[place * high : (place + 1) * high]

    if len(rest) == 3:
        multiply()
        return
    square_ref = rest[0]
    step = pl.program_id(0)
    pl.when(step < tiles)(multiply)

    @pl.when(step == tiles)
    def squares():
        for place, home in enumerate(homes):
            home[0, :, 0:128] = square_ref[place].astype(BF16)
            home[1, :, 0:128] = jnp.zeros((high, 128), BF16)


def gate_up(scaled, gate_weight, up_weight, width, squares=None):
    depth, rows = scaled.shape
    high = rows // 4
    tiles = pl.cdiv(width, TILE)
    weight = pl.BlockSpec((TILE, depth), lambda j: (jnp.minimum(j, tiles - 1), 0))
    piece = pl.BlockSpec((2, high, TILE), lambda j: (0, 0, j))
    ins = [scaled, gate_weight, up_weight]
    specs = [whole(scaled.shape), weight, weight]
    if squares is not None:
        ins.append(squares)
        specs.append(whole(squares.shape))
        width += 128
    return pl.pallas_call(
        functools.partial(gate_up_kernel, tiles),
        grid=(tiles + len(ins) - 3,),
        in_specs=specs,
        out_specs=[piece, piece, pl.BlockSpec((2, 2, high, TILE), lambda j: (0, 0, 0, j))],
        out_shape=[
            jax.ShapeDtypeStruct((2, high, width), BF16),
            jax.ShapeDtypeStruct((2, high, width), BF16),
            jax.ShapeDtypeStruct((2, 2, high, width), BF16),
        ],
        compiler_params=params(),
        cost_estimate=cost(4 * rows * depth * width, 4 * depth * width),
    )(*ins)


def activate_kernel(model, width, own_norm, keep_ref, got_ref, crossed_ref, *rest):
    def total(which, low, high):
        value = keep_ref[which, :, low:high].astype(F32)
        value += got_ref[0, which, :, low:high].astype(F32)
        return value + crossed_ref[which, :, low:high].astype(F32)

    if own_norm:
        hidden_ref, norm_ref = rest[-2:]
        squares = jnp.sum(total(0, width, width + 128), axis=1, keepdims=True)
        norm = lax.rsqrt(squares / model + 1e-06)
        norm_ref[...] = jnp.broadcast_to(norm, norm_ref.shape)
    else:
        hidden_ref = rest[-1]
        norm = rest[0][:, 0:1]
    gate = total(0, 0, width) * norm
    up = total(1, 0, width) * norm
    hidden_ref[...] = (gate / (1.0 + jnp.exp(-gate)) * up).astype(BF16)


def activate(model, width, keep, got, crossed, norm, *behind):
    high = keep.shape[1]
    shapes = [jax.ShapeDtypeStruct((high, width), BF16)]
    if norm is None:
        shapes.append(jax.ShapeDtypeStruct((high, 128), F32))
    ins = [keep, got, crossed] + ([] if norm is None else [norm]) + list(behind)
    result = pl.pallas_call(
        functools.partial(activate_kernel, model, width, norm is None),
        out_shape=shapes,
        compiler_params=params(),
        cost_estimate=cost(20 * high * width, 14 * high * width, high * width),
    )(*ins)
    return result if norm is None else (result[0], norm)


def down_kernel(width, slots, has_start, last, scalars, *refs):
    hidden = refs[0:4]
    weight_ref = refs[4]
    rest = list(refs[5:])
    start_ref = rest.pop(0) if has_start else None
    acc, packed = rest[-2], rest[-1]
    outs = rest[:-2]
    step = pl.program_id(0)
    depth = weight_ref.shape[0]
    high = hidden[0].shape[0]
    steps = pl.num_programs(0)

    @pl.when(step == 0)
    def begin():
        if width % depth:
            packed[...] = jnp.zeros_like(packed)
        for place in range(4):
            packed[place * high : (place + 1) * high, 0:width] = hidden[place][...]
        if has_start:
            acc[...] = start_ref[...]
        else:
            acc[...] = jnp.zeros_like(acc)

    start = pl.multiple_of(step * depth, depth)

    def add(weight):
        term = jnp.dot(packed[:, pl.ds(start, depth)], weight, preferred_element_type=F32)
        acc[...] += term.reshape(acc.shape)

    if width % depth:

        @pl.when(step < steps - 1)
        def inner():
            add(weight_ref[...])

        @pl.when(step == steps - 1)
        def edge():
            row = lax.broadcasted_iota(jnp.int32, weight_ref.shape, 0)
            add(jnp.where(row < width % depth, weight_ref[...], jnp.zeros_like(weight_ref)))
    else:
        add(weight_ref[...])

    @pl.when(step == steps - 1)
    def finish():
        if not last:
            outs[0][...] = acc[...]
            return
        rows = high // slots
        for k in range(4):
            place = swapped_bits(scalars[5] ^ k)
            block = acc[place]
            for s in range(slots):
                out = outs[k * slots + s]
                out[...] = block[s * rows : (s + 1) * rows].astype(out.dtype)


def down(scalars, hidden, down_weight, start, slots, last):
    high, width = hidden[0].shape
    cols = down_weight.shape[1]
    steps = pl.cdiv(width, TILE)
    rows = high // slots
    ins = [whole((high, width))] * 4 + [pl.BlockSpec((TILE, cols), lambda i, s: (i, 0))]
    args = list(hidden) + [down_weight]
    if start is not None:
        ins.append(whole((4, high, cols)))
        args.append(start)
    if last:
        shapes = [
            jax.ShapeDtypeStruct((rows, cols), F32 if s == 0 else BF16)
            for k in range(4)
            for s in range(slots)
        ]
    else:
        shapes = [jax.ShapeDtypeStruct((4, high, cols), F32)]
    return pl.pallas_call(
        functools.partial(down_kernel, width, slots, start is not None, last),
        grid_spec=pltpu.PrefetchScalarGridSpec(
            num_scalar_prefetch=1,
            grid=(steps,),
            in_specs=ins,
            out_specs=[whole(shape.shape) for shape in shapes],
            scratch_shapes=[
                pltpu.VMEM((4, high, cols), F32),
                pltpu.VMEM((4 * high, steps * TILE), BF16),
            ],
        ),
        out_shape=shapes,
        compiler_params=params(),
        cost_estimate=cost(8 * high * width * cols, 2 * width * cols),
    )(scalars, *args)


def to_core(x):
    return lax.ppermute(x, "ffn", [(i, i ^ 1) for i in range(4)])


def to_x(x):
    return lax.ppermute(x, "ffn", [(i, i ^ 2) for i in range(4)])


def to_z(x, k):
    return lax.ppermute(x, "tp", [(i, i ^ k) for i in range(4)])


def to_y(x):
    return lax.ppermute(x, "grp", [(0, 1), (1, 0)])


def cut(total):
    edges = [0]
    for tiles in CHUNKS:
        edges.append(min(edges[-1] + tiles * TILE, total))
    return [(low, high - low) for low, high in zip(edges, edges[1:])]


def body(
    queries,
    new_kv,
    kv_cache,
    lengths,
    prefixes,
    resid,
    out_weight,
    gain,
    gate_weight,
    up_weight,
    down_weight,
):
    span = queries.shape[0]
    local_kv = new_kv.shape[2] // DH
    cache_len = kv_cache.shape[2]
    groups = lax.axis_size("grp")
    tp_size = lax.axis_size("tp")
    g, t, f = lax.axis_index("grp"), lax.axis_index("tp"), lax.axis_index("ffn")
    core = f & 1
    length = lengths[0]
    rows = span // tp_size
    model = gain.shape[0] * lax.axis_size("ffn")
    usable = jnp.clip(prefixes[0] - f * cache_len, 0, cache_len)
    first = (f == 0).astype(jnp.int32)
    scalars = jnp.stack([core, usable, length, first, t, t ^ f]).astype(jnp.int32)
    scalars = lax.optimization_barrier(scalars)
    sent, kept, sent_lse, kept_lse = attention(scalars, queries, kv_cache, new_kv)
    got, got_lse = to_core(sent), to_core(sent_lse)
    kept, kept_lse = combine(kept, got, kept_lse, got_lse)
    (out_held,), mark, kept = fetch([out_weight], [(0, out_weight.shape[0])], kept)
    got, got_lse = to_x(kept), to_x(kept_lse)
    mine, unused = combine(kept, got, kept_lse, got_lse, mark)
    other = to_core(mine)

    terms = list(project(scalars, mine, other, out_held, tp_size))
    chunks = cut(gate_weight.shape[1])
    pair = [gate_weight.T, up_weight.T]
    (gate0, up0, gate1), mark, terms[1] = fetch(
        pair + pair[:1], [chunks[0], chunks[0], chunks[1]], terms[1]
    )
    passed = [to_z(terms[k], k) for k in (1, 3, 2)]
    h1 = add_residual(scalars, resid, terms[0], passed, mark)

    natural = g ^ jnp.arange(groups, dtype=jnp.int32)
    by_z = [h1, to_z(h1, 1), to_z(h1, 2)]
    across = None
    if groups == 2:
        by_z[2], across = lax.optimization_barrier((by_z[2], to_y(h1)))
    by_z.append(to_z(by_z[2], 1))
    (up1,), mark, by_z[1] = fetch(pair[1:], chunks[1:], by_z[1])
    held = [(gate0, up0), (gate1, up1)]
    sources = []
    for part in by_z:
        if groups == 2:
            sources += [part, to_y(part) if sources else across]
        else:
            everyone = jnp.take(lax.all_gather(part, "grp"), natural, axis=0)
            sources += [everyone[s] for s in range(groups)]
    scaled, squares = scale_rows(scalars, sources, gain[None, :], mark)

    reduced = []
    for index, (begin, width) in enumerate(chunks):
        extra = squares if begin == 0 else None
        keep, cross, send = gate_up(scaled, *held[index], width, extra)
        if index == 0:
            scaled, send = lax.optimization_barrier((scaled, send))
        got = to_core(send)
        cross = (cross.astype(F32) + got[1].astype(F32)).astype(BF16)
        if index == 1:
            held, mark, cross = fetch([down_weight] * 2, chunks, cross)
        reduced.append((keep, got, to_x(cross)))
    first, second = (width for begin, width in chunks)
    hidden, norm = activate(model, first, *reduced[0], None, mark)
    over, near = to_x(hidden), to_core(hidden)
    later, norm = activate(model, second, *reduced[1], norm, hidden)
    far = to_x(later)
    over, later = lax.optimization_barrier((over, later))
    pieces = [hidden, over, near, to_core(over)]
    (total,) = down(scalars, pieces, held[0], None, groups, False)
    far, total = lax.optimization_barrier((far, total))
    pieces = [later, far, to_core(later), to_core(far)]
    result = down(scalars, pieces, held[1], total, groups, True)

    chunk_sums = []
    for k in range(4):
        own = result[k * groups]
        others = result[k * groups + 1 : (k + 1) * groups]
        if groups == 2:
            chunk_sums.append((own, others[0]))
        else:
            stacked = jnp.stack([own.astype(BF16)] + list(others))
            stacked = jnp.take(stacked, natural, axis=0)
            moved = lax.all_to_all(stacked, "grp", split_axis=0, concat_axis=0, tiled=True)
            chunk_sums.append(jnp.sum(moved.astype(F32), axis=0))
    parts = [h1]
    for k in (3, 2, 1, 0):
        if groups == 2:
            own, away = chunk_sums[k]
            away = to_y(away)
            if k == 0:
                parts += [own, away]
                continue
            value = own + away.astype(F32)
        else:
            value = chunk_sums[k]
        parts.append(value if k == 0 else to_z(value.astype(BF16), k))
    total = sum(part.astype(F32) for part in parts)
    live = t * rows + jnp.arange(rows, dtype=jnp.int32) < length
    return jnp.where(live[:, None], total, 0.0).astype(BF16)


def merged(x, axis, combine):
    everything = jax.tree.map(lambda part: lax.all_gather(part, axis), x)
    leading = jax.tree.map(lambda part: part[0], everything)

    def hop(k, so_far):
        return combine(so_far, jax.tree.map(lambda part: part[k], everything))

    return lax.fori_loop(1, lax.axis_size(axis), hop, leading)


def combine_parts(first, second):
    top = jnp.maximum(first[0], second[0])
    left = jnp.exp(first[0] - top)
    right = jnp.exp(second[0] - top)
    total = first[1] * left + second[1] * right
    values = first[2] * left[..., None] + second[2] * right[..., None]
    return (top, total, values)


def general_body(
    queries,
    new_kv,
    kv_cache,
    lengths,
    prefixes,
    resid,
    out_weight,
    gain,
    gate_weight,
    up_weight,
    down_weight,
):
    span, qcols = queries.shape
    kcols = new_kv.shape[2]
    local_kv = kcols // DH
    group = qcols // DH // local_kv
    cache_len = kv_cache.shape[2]
    length = lengths[0]
    model = gain.shape[0] * lax.axis_size("ffn")
    prefix = prefixes[0]
    width_index = lax.axis_index("ffn")
    shard_start = width_index * cache_len
    query_heads = (
        queries.reshape(span, local_kv, group, DH)
        .transpose(1, 2, 0, 3)
        .reshape(local_kv, group * span, DH)
    )
    row_pos = jnp.tile(jnp.arange(span, dtype=jnp.int32), group)
    inv_scale = 1.0 / math.sqrt(DH)

    def update(state, keys, values, valid):
        top, total, acc = state
        scores = (
            jnp.einsum("hrd,hkd->hrk", query_heads, keys, preferred_element_type=jnp.float32)
            * inv_scale
        )
        scores = jnp.where(valid[None], scores, NEGATIVE)
        new_top = jnp.maximum(top, jnp.max(scores, axis=-1))
        probs = jnp.where(valid[None], jnp.exp(scores - new_top[..., None]), 0.0)
        factor = jnp.exp(top - new_top)
        total = total * factor + jnp.sum(probs, axis=-1)
        acc = acc * factor[..., None] + jnp.einsum(
            "hrk,hkd->hrd", probs, values.astype(jnp.float32)
        )
        return (new_top, total, acc)

    block = math.gcd(512, cache_len)
    blocks = cache_len // block
    cache_keys = kv_cache[0, 0].reshape(blocks, block, local_kv, DH).transpose(0, 2, 1, 3)
    cache_values = kv_cache[1, 0].reshape(blocks, block, local_kv, DH).transpose(0, 2, 1, 3)
    rows = group * span
    start_state = (
        jnp.full((local_kv, rows), NEGATIVE, jnp.float32),
        jnp.zeros((local_kv, rows), jnp.float32),
        jnp.zeros((local_kv, rows, DH), jnp.float32),
    )

    def cache_step(state, items):
        keys, values, index = items
        positions = shard_start + index * block + jnp.arange(block, dtype=jnp.int32)
        valid = jnp.broadcast_to((positions < prefix)[None, :], (rows, block))
        return (update(state, keys, values, valid), None)

    state, unused = lax.scan(
        cache_step, start_state, (cache_keys, cache_values, jnp.arange(blocks, dtype=jnp.int32))
    )
    block_keys = new_kv[0].reshape(span, local_kv, DH).transpose(1, 0, 2)
    block_values = new_kv[1].reshape(span, local_kv, DH).transpose(1, 0, 2)
    slots = jnp.arange(span, dtype=jnp.int32)[None, :]
    new_valid = (slots < length) & (slots <= row_pos[:, None]) & (width_index == 0)
    state = update(state, block_keys, block_values, new_valid)
    top, total, acc = merged(state, "ffn", combine_parts)
    heads = acc / total[..., None]
    attn = (
        heads.reshape(local_kv, group, span, DH)
        .transpose(2, 0, 1, 3)
        .reshape(span, qcols)
        .astype(jnp.bfloat16)
    )
    partial_value = jnp.dot(attn, out_weight, preferred_element_type=jnp.float32)
    summed = lax.psum(partial_value, "tp")
    h1 = (summed + resid.astype(jnp.float32)).astype(jnp.bfloat16)
    all_rows = lax.all_gather(h1, "grp", axis=0, tiled=True)
    rows_f = all_rows.astype(jnp.float32)
    squares = jnp.sum(rows_f * rows_f, axis=1)
    scaled = (rows_f * gain.astype(jnp.float32)[None, :]).astype(jnp.bfloat16)
    gate = jnp.dot(scaled, gate_weight, preferred_element_type=jnp.float32)
    upper = jnp.dot(scaled, up_weight, preferred_element_type=jnp.float32)
    rows_here = span // lax.axis_size("tp")
    gate, upper, squares = lax.psum((gate, upper, squares), "ffn")
    inv_rms = lax.rsqrt(squares / model + 1e-06)
    hidden = (jax.nn.silu(gate * inv_rms[:, None]) * (upper * inv_rms[:, None])).astype(
        jnp.bfloat16
    )
    down_rows = lax.psum_scatter(
        jnp.dot(hidden, down_weight, preferred_element_type=jnp.float32),
        ("grp", "tp"),
        scatter_dimension=0,
        tiled=True,
    )
    row_start = lax.axis_index("tp") * rows_here
    own = lax.dynamic_slice_in_dim(h1, row_start, rows_here, 0)
    live = row_start + jnp.arange(rows_here, dtype=jnp.int32) < length
    return jnp.where(live[:, None], own.astype(jnp.float32) + down_rows, 0.0).astype(jnp.bfloat16)


def solution(mesh):
    sizes = tuple(mesh.shape[axis] for axis in ("grp", "tp", "ffn"))
    return jax.shard_map(
        body if sizes == (2, 4, 4) else general_body,
        mesh=mesh,
        in_specs=(
            P("grp", "tp"),
            P(None, "grp", "tp"),
            P(None, "grp", "ffn", "tp"),
            P("grp"),
            P("grp"),
            P("grp", "ffn"),
            P("tp", "ffn"),
            P("ffn"),
            P("ffn", ("grp", "tp")),
            P("ffn", ("grp", "tp")),
            P(("grp", "tp"), "ffn"),
        ),
        out_specs=P(("grp", "tp"), "ffn"),
        check_vma=False,
    )
```

```python
import functools
import math

import jax
import jax.numpy as jnp
from jax import lax
from jax.experimental import pallas as pl
from jax.experimental.pallas import tpu as pltpu
from jax.sharding import PartitionSpec as P

DH = 128
TILE = 640
CHUNKS = (3, 3)
HEADS = 4
THIN = 1
NEGATIVE = -1e30
BF16 = jnp.bfloat16
F32 = jnp.float32
LIMIT = 8 * 1024 * 1024
ORDER = (0, 2, 1, 3)


def swapped_bits(index):
    return (index & 1) * 2 + (index >> 1)


def params(limit=LIMIT):
    return pltpu.CompilerParams(vmem_limit_bytes=limit)


def cost(flops, moved, exps=0):
    return pl.CostEstimate(
        flops=int(flops) // THIN, bytes_accessed=int(moved) // THIN, transcendentals=int(exps) // THIN
    )


def whole(shape):
    return pl.BlockSpec(shape, lambda *unused: (0,) * len(shape))


def fetch_kernel(pieces, *refs):
    count = len(pieces)
    sources, targets, mark, done = refs[:count], refs[count : 2 * count], refs[-2], refs[-1]
    copies = []
    for i, (begin, width) in enumerate(pieces):
        source = sources[i].at[pl.ds(begin, width)]
        copies.append(pltpu.make_async_copy(source, targets[i], done.at[i]))
    for copy in copies:
        copy.start()
    mark[...] = jnp.zeros_like(mark)
    for copy in copies:
        copy.wait()


def fetch(weights, pieces, after):
    *weights, after = lax.optimization_barrier((*weights, after))
    weights = [pltpu.with_memory_space_constraint(weight, pltpu.HBM) for weight in weights]
    shapes = [
        jax.ShapeDtypeStruct((width, weight.shape[1]), weight.dtype)
        for weight, (begin, width) in zip(weights, pieces)
    ]
    *held, mark = pl.pallas_call(
        functools.partial(fetch_kernel, pieces),
        in_specs=[pl.BlockSpec(memory_space=pltpu.HBM)] * len(weights),
        out_specs=[pl.BlockSpec(memory_space=pltpu.VMEM)] * (len(weights) + 1),
        out_shape=shapes + [jax.ShapeDtypeStruct((8, 128), F32)],
        scratch_shapes=[pltpu.SemaphoreType.DMA((len(weights),))],
        compiler_params=params(),
        cost_estimate=cost(0, 4 * sum(shape.size for shape in shapes)),
    )(*weights)
    return held, mark, after


def attention_kernel(
    scalars, q_ref, key_ref, value_ref, new_key_ref, new_value_ref, sent_ref, kept_ref, sent_lse_ref, kept_lse_ref, columns
):
    step = pl.program_id(0)
    span = q_ref.shape[0]
    cache_len = key_ref.shape[2]
    per_kv = sent_lse_ref.shape[0]
    usable, length, first = scalars[1], scalars[2], scalars[3]
    scale = 1.0 / math.sqrt(DH)
    position = lax.broadcasted_iota(jnp.int32, (1, cache_len), 1)
    bias = jnp.where(position < usable, 0.0, NEGATIVE)
    row = lax.broadcasted_iota(jnp.int32, (span, span), 0)
    col = lax.broadcasted_iota(jnp.int32, (span, span), 1)
    allowed = (col <= row) & (col < length) & (first > 0)
    fresh_bias = jnp.concatenate([jnp.where(allowed, 0.0, NEGATIVE)] * HEADS, axis=0)
    contract = (((1,), (1,)), ((), ()))
    keys, values = key_ref[0, 0], value_ref[0, 0]
    new_keys, new_values = new_key_ref[0], new_value_ref[0]
    columns[...] = jnp.zeros_like(columns)
    for low in range(0, per_kv, HEADS):
        heads = range(low, low + HEADS)
        q = jnp.concatenate([q_ref[:, h * DH : (h + 1) * DH] for h in heads], axis=0)
        scores = lax.dot_general(q, keys, contract, preferred_element_type=F32) * scale + bias
        fresh = lax.dot_general(q, new_keys, contract, preferred_element_type=F32)
        fresh = fresh * scale + fresh_bias
        top = jnp.maximum(
            jnp.max(scores, axis=1, keepdims=True), jnp.max(fresh, axis=1, keepdims=True)
        )
        probs = jnp.exp(scores - top)
        fresh_probs = jnp.exp(fresh - top)
        total = jnp.sum(probs, axis=1, keepdims=True) + jnp.sum(fresh_probs, axis=1, keepdims=True)
        mixed = jnp.dot(probs.astype(BF16), values, preferred_element_type=F32)
        mixed += jnp.dot(fresh_probs.astype(BF16), new_values, preferred_element_type=F32)
        mixed = (mixed / total).astype(BF16)
        lse = top + jnp.log(total)
        for i, h in enumerate(heads):
            columns[0:span, h : h + 1] = lse[i * span : (i + 1) * span]
            piece = mixed[i * span : (i + 1) * span]

            @pl.when(step == 0)
            def to_sent():
                sent_ref[:, h * DH : (h + 1) * DH] = piece

            @pl.when(step == 1)
            def to_kept():
                kept_ref[:, h * DH : (h + 1) * DH] = piece

    rows = jnp.transpose(columns[...])[0:per_kv, :]

    @pl.when(step == 0)
    def lse_sent():
        sent_lse_ref[...] = rows

    @pl.when(step == 1)
    def lse_kept():
        kept_lse_ref[...] = rows


def attention(scalars, queries, kv_cache, new_kv):
    span, qcols = queries.shape
    per_kv = qcols // DH // 2
    cache_len = kv_cache.shape[2]
    width = per_kv * DH

    def which(i, s):
        return s[0] ^ 1 ^ i

    def at_home(array):
        return pltpu.with_memory_space_constraint(array, pltpu.HBM)

    call = pl.pallas_call(
        attention_kernel,
        grid_spec=pltpu.PrefetchScalarGridSpec(
            num_scalar_prefetch=1,
            grid=(2,),
            in_specs=[
                pl.BlockSpec((span, width), lambda i, s: (0, which(i, s))),
                pl.BlockSpec((1, 1, cache_len, DH), lambda i, s: (0, 0, 0, which(i, s))),
                pl.BlockSpec((1, 1, cache_len, DH), lambda i, s: (1, 0, 0, which(i, s))),
                pl.BlockSpec((1, span, DH), lambda i, s: (0, 0, which(i, s))),
                pl.BlockSpec((1, span, DH), lambda i, s: (1, 0, which(i, s))),
            ],
            out_specs=[whole((span, width))] * 2 + [whole((per_kv, 128))] * 2,
            scratch_shapes=[pltpu.VMEM((128, 128), F32)],
        ),
        out_shape=[jax.ShapeDtypeStruct((span, width), BF16)] * 2
        + [jax.ShapeDtypeStruct((per_kv, 128), F32)] * 2,
        compiler_params=params(40 * 1024 * 1024),
        cost_estimate=cost(
            8 * span * per_kv * cache_len * DH, 8 * cache_len * DH, 2 * span * per_kv * cache_len
        ),
    )
    queries, kv_cache, new_kv = at_home(queries), at_home(kv_cache), at_home(new_kv)
    return call(scalars, queries, kv_cache, kv_cache, new_kv, new_kv)


def combine_kernel(a_ref, b_ref, lse_a_ref, lse_b_ref, *rest):
    out_ref, lse_ref = rest[-2:]
    span = a_ref.shape[0]
    heads = lse_a_ref.shape[0]
    lse_a, lse_b = lse_a_ref[...], lse_b_ref[...]
    top = jnp.maximum(lse_a, lse_b)
    left, right = jnp.exp(lse_a - top), jnp.exp(lse_b - top)
    total = left + right
    lse_ref[...] = top + jnp.log(total)
    rest = jnp.zeros((128 - 2 * heads, 128), F32)
    table = jnp.transpose(jnp.concatenate([left / total, right / total, rest], axis=0))
    for h in range(heads):
        cols = slice(h * DH, (h + 1) * DH)
        mixed = a_ref[:, cols].astype(F32) * table[0:span, h : h + 1]
        mixed += b_ref[:, cols].astype(F32) * table[0:span, heads + h : heads + h + 1]
        out_ref[:, cols] = mixed.astype(BF16)


def combine(a, b, lse_a, lse_b, *behind):
    return pl.pallas_call(
        combine_kernel,
        out_shape=[
            jax.ShapeDtypeStruct(a.shape, BF16),
            jax.ShapeDtypeStruct(lse_a.shape, F32),
        ],
        compiler_params=params(),
        cost_estimate=cost(4 * a.size, 6 * a.size),
    )(a, b, lse_a, lse_b, *behind)


def project_kernel(scalars, keep_ref, other_ref, weight_ref, *rest):
    outs, acc = rest[:-1], rest[-1]
    step = pl.program_id(0)
    depth = weight_ref.shape[0]
    half = pl.num_programs(0) // 2
    rows = outs[0].shape[0]

    @pl.when(step < half)
    def from_keep():
        start = pl.multiple_of(step * depth, depth)
        term = jnp.dot(keep_ref[:, pl.ds(start, depth)], weight_ref[...], preferred_element_type=F32)

        @pl.when(step == 0)
        def begin():
            acc[...] = term

        @pl.when(step > 0)
        def go_on():
            acc[...] += term

    @pl.when(step >= half)
    def from_other():
        start = pl.multiple_of((step - half) * depth, depth)
        acc[...] += jnp.dot(
            other_ref[:, pl.ds(start, depth)], weight_ref[...], preferred_element_type=F32
        )

    @pl.when(step == pl.num_programs(0) - 1)
    def finish():
        for k, out in enumerate(outs):
            start = pl.multiple_of((scalars[4] ^ k) * rows, 8)
            out[...] = acc[pl.ds(start, rows), :].astype(out.dtype)


def project(scalars, keep, other, out_weight, tp_size):
    span, width = keep.shape
    depth = 512
    half = width // depth
    cols = out_weight.shape[1]
    rows = span // tp_size
    return pl.pallas_call(
        project_kernel,
        grid_spec=pltpu.PrefetchScalarGridSpec(
            num_scalar_prefetch=1,
            grid=(2 * half,),
            in_specs=[
                whole((span, width)),
                whole((span, width)),
                pl.BlockSpec(
                    (depth, cols),
                    lambda i, s: (jnp.where(i < half, s[0], 1 - s[0]) * half + i % half, 0),
                ),
            ],
            out_specs=[whole((rows, cols))] * tp_size,
            scratch_shapes=[pltpu.VMEM((span, cols), F32)],
        ),
        out_shape=[
            jax.ShapeDtypeStruct((rows, cols), F32 if k == 0 else BF16) for k in range(tp_size)
        ],
        compiler_params=params(),
        cost_estimate=cost(4 * span * width * cols, 4 * width * cols),
    )(scalars, keep, other, out_weight)


def residual_kernel(scalars, resid_ref, first_ref, *rest):
    out_ref, spread = rest[-2:]
    rows = out_ref.shape[0]
    spread[...] = resid_ref[...].astype(F32)
    total = first_ref[...] + spread[pl.ds(pl.multiple_of(scalars[4] * rows, 8), rows), :]
    for term in rest[:3]:
        total += term[...].astype(F32)
    out_ref[...] = total.astype(BF16)


def add_residual(scalars, resid, first, others, *behind):
    shape = first.shape
    ins = [resid, first, *others, *behind]
    return pl.pallas_call(
        residual_kernel,
        grid_spec=pltpu.PrefetchScalarGridSpec(
            num_scalar_prefetch=1,
            grid=(1,),
            in_specs=[whole(part.shape) for part in ins],
            out_specs=whole(shape),
            scratch_shapes=[pltpu.VMEM(resid.shape, F32)],
        ),
        out_shape=jax.ShapeDtypeStruct(shape, BF16),
        compiler_params=params(),
        cost_estimate=cost(5 * first.size, 12 * first.size),
    )(scalars, *ins)


def scale_kernel(slots, scalars, *refs):
    count = 4 * slots
    sources, gain_ref = refs[:count], refs[count]
    scaled_ref, square_ref, ordered = refs[-3:]
    gain = gain_ref[...].astype(F32)
    cols = gain.shape[1]
    for k in range(4):
        place = swapped_bits(scalars[5] ^ k)
        rows = jnp.concatenate(
            [sources[k * slots + s][...].astype(F32) for s in range(slots)], axis=0
        )
        ordered[place] = rows * gain
        squares = rows * rows
        part = squares[:, 0:128]
        for c in range(128, cols, 128):
            part += squares[:, c : c + 128]
        square_ref[place] = part
    tall = ordered[...].reshape(scaled_ref.shape[1], cols)
    scaled_ref[...] = jnp.transpose(tall).astype(BF16)


def scale_rows(scalars, sources, gain, mark):
    slots = len(sources) // 4
    rows, cols = sources[0].shape
    high = rows * slots
    return pl.pallas_call(
        functools.partial(scale_kernel, slots),
        grid_spec=pltpu.PrefetchScalarGridSpec(
            num_scalar_prefetch=1,
            grid=(1,),
            in_specs=[whole((rows, cols))] * len(sources) + [whole((1, cols)), whole(mark.shape)],
            out_specs=[whole((cols, 4 * high)), whole((4, high, 128))],
            scratch_shapes=[pltpu.VMEM((4, high, cols), F32)],
        ),
        out_shape=[
            jax.ShapeDtypeStruct((cols, 4 * high), BF16),
            jax.ShapeDtypeStruct((4, high, 128), F32),
        ],
        compiler_params=params(),
        cost_estimate=cost(4 * 4 * high * cols, 4 * 4 * high * cols),
    )(scalars, *sources, gain, mark)


def gate_up_kernel(tiles, scaled_ref, gate_ref, up_ref, *rest):
    homes = rest[-4:]
    high = homes[0].shape[1]

    def multiply():
        for which, weight in enumerate((gate_ref, up_ref)):
            term = jnp.dot(weight[...], scaled_ref[...], preferred_element_type=F32)
            term = jnp.transpose(term).astype(BF16)
            for place, home in enumerate(homes):
                home[which] = term[place * high : (place + 1) * high]

    if len(rest) == 4:
        multiply()
        return
    square_ref = rest[0]
    step = pl.program_id(0)
    pl.when(step < tiles)(multiply)

    @pl.when(step == tiles)
    def squares():
        for place, home in enumerate(homes):
            home[0, :, 0:128] = square_ref[place].astype(BF16)
            home[1, :, 0:128] = jnp.zeros((high, 128), BF16)


def gate_up(scaled, gate_weight, up_weight, width, squares=None):
    depth, rows = scaled.shape
    high = rows // 4
    tiles = pl.cdiv(width, TILE)
    weight = pl.BlockSpec((TILE, depth), lambda j: (jnp.minimum(j, tiles - 1), 0))
    piece = pl.BlockSpec((2, high, TILE), lambda j: (0, 0, j))
    ins = [scaled, gate_weight, up_weight]
    specs = [whole(scaled.shape), weight, weight]
    if squares is not None:
        ins.append(squares)
        specs.append(whole(squares.shape))
        width += 128
    return pl.pallas_call(
        functools.partial(gate_up_kernel, tiles),
        grid=(tiles + len(ins) - 3,),
        in_specs=specs,
        out_specs=[piece] * 4,
        out_shape=[jax.ShapeDtypeStruct((2, high, width), BF16)] * 4,
        compiler_params=params(),
        cost_estimate=cost(4 * rows * depth * width, 4 * depth * width),
    )(*ins)


def activate_kernel(model, width, own_norm, keep_ref, got_ref, crossed_ref, *rest):
    def total(which, low, high):
        value = keep_ref[which, :, low:high].astype(F32)
        value += got_ref[which, :, low:high].astype(F32)
        return value + crossed_ref[which, :, low:high].astype(F32)

    if own_norm:
        hidden_ref, norm_ref = rest[-2:]
        squares = jnp.sum(total(0, width, width + 128), axis=1, keepdims=True)
        norm = lax.rsqrt(squares / model + 1e-06)
        norm_ref[...] = jnp.broadcast_to(norm, norm_ref.shape)
    else:
        hidden_ref = rest[-1]
        norm = rest[0][:, 0:1]
    gate = total(0, 0, width) * norm
    up = total(1, 0, width) * norm
    hidden_ref[...] = (gate / (1.0 + jnp.exp(-gate)) * up).astype(BF16)


def activate(model, width, keep, got, crossed, norm, *behind):
    high = keep.shape[1]
    shapes = [jax.ShapeDtypeStruct((high, width), BF16)]
    if norm is None:
        shapes.append(jax.ShapeDtypeStruct((high, 128), F32))
    ins = [keep, got, crossed] + ([] if norm is None else [norm]) + list(behind)
    result = pl.pallas_call(
        functools.partial(activate_kernel, model, width, norm is None),
        out_shape=shapes,
        compiler_params=params(),
        cost_estimate=cost(20 * high * width, 14 * high * width, high * width),
    )(*ins)
    return result if norm is None else (result[0], norm)


def down_kernel(width, slots, has_start, last, scalars, *refs):
    hidden = refs[0:4]
    weight_ref = refs[4]
    rest = list(refs[5:])
    start_ref = rest.pop(0) if has_start else None
    acc, packed = rest[-2], rest[-1]
    outs = rest[:-2]
    step = pl.program_id(0)
    depth = weight_ref.shape[0]
    high = hidden[0].shape[0]
    steps = pl.num_programs(0)

    @pl.when(step == 0)
    def begin():
        if width % depth:
            packed[...] = jnp.zeros_like(packed)
        for place in range(4):
            packed[place * high : (place + 1) * high, 0:width] = hidden[place][...]
        if has_start:
            acc[...] = start_ref[...]
        else:
            acc[...] = jnp.zeros_like(acc)

    start = pl.multiple_of(step * depth, depth)

    def add(weight):
        term = jnp.dot(packed[:, pl.ds(start, depth)], weight, preferred_element_type=F32)
        acc[...] += term.reshape(acc.shape)

    if width % depth:

        @pl.when(step < steps - 1)
        def inner():
            add(weight_ref[...])

        @pl.when(step == steps - 1)
        def edge():
            row = lax.broadcasted_iota(jnp.int32, weight_ref.shape, 0)
            add(jnp.where(row < width % depth, weight_ref[...], jnp.zeros_like(weight_ref)))
    else:
        add(weight_ref[...])

    @pl.when(step == steps - 1)
    def finish():
        if not last:
            outs[0][...] = acc[...]
            return
        rows = high // slots
        for k in range(4):
            place = swapped_bits(scalars[5] ^ k)
            block = acc[place]
            for s in range(slots):
                out = outs[k * slots + s]
                out[...] = block[s * rows : (s + 1) * rows].astype(out.dtype)


def down(scalars, hidden, down_weight, start, slots, last):
    high, width = hidden[0].shape
    cols = down_weight.shape[1]
    steps = pl.cdiv(width, TILE)
    rows = high // slots
    ins = [whole((high, width))] * 4 + [pl.BlockSpec((TILE, cols), lambda i, s: (i, 0))]
    args = list(hidden) + [down_weight]
    if start is not None:
        ins.append(whole((4, high, cols)))
        args.append(start)
    if last:
        shapes = [
            jax.ShapeDtypeStruct((rows, cols), F32 if s == 0 else BF16)
            for k in range(4)
            for s in range(slots)
        ]
    else:
        shapes = [jax.ShapeDtypeStruct((4, high, cols), F32)]
    return pl.pallas_call(
        functools.partial(down_kernel, width, slots, start is not None, last),
        grid_spec=pltpu.PrefetchScalarGridSpec(
            num_scalar_prefetch=1,
            grid=(steps,),
            in_specs=ins,
            out_specs=[whole(shape.shape) for shape in shapes],
            scratch_shapes=[
                pltpu.VMEM((4, high, cols), F32),
                pltpu.VMEM((4 * high, steps * TILE), BF16),
            ],
        ),
        out_shape=shapes,
        compiler_params=params(),
        cost_estimate=cost(8 * high * width * cols, 2 * width * cols),
    )(scalars, *args)


def to_core(x):
    return lax.ppermute(x, "ffn", [(i, i ^ 1) for i in range(4)])


def to_x(x):
    return lax.ppermute(x, "ffn", [(i, i ^ 2) for i in range(4)])


def to_z(x, k):
    return lax.ppermute(x, "tp", [(i, i ^ k) for i in range(4)])


def to_y(x):
    return lax.ppermute(x, "grp", [(0, 1), (1, 0)])


def cut(total):
    edges = [0]
    for tiles in CHUNKS:
        edges.append(min(edges[-1] + tiles * TILE, total))
    return [(low, high - low) for low, high in zip(edges, edges[1:])]


def body(
    queries,
    new_kv,
    kv_cache,
    lengths,
    prefixes,
    resid,
    out_weight,
    gain,
    gate_weight,
    up_weight,
    down_weight,
):
    span = queries.shape[0]
    local_kv = new_kv.shape[2] // DH
    cache_len = kv_cache.shape[2]
    groups = lax.axis_size("grp")
    tp_size = lax.axis_size("tp")
    g, t, f = lax.axis_index("grp"), lax.axis_index("tp"), lax.axis_index("ffn")
    core = f & 1
    length = lengths[0]
    rows = span // tp_size
    model = gain.shape[0] * lax.axis_size("ffn")
    usable = jnp.clip(prefixes[0] - f * cache_len, 0, cache_len)
    first = (f == 0).astype(jnp.int32)
    scalars = jnp.stack([core, usable, length, first, t, t ^ f]).astype(jnp.int32)
    scalars = lax.optimization_barrier(scalars)
    sent, kept, sent_lse, kept_lse = attention(scalars, queries, kv_cache, new_kv)
    got, got_lse = to_core(sent), to_core(sent_lse)
    kept, kept_lse = combine(kept, got, kept_lse, got_lse)
    (out_held,), mark, kept = fetch([out_weight], [(0, out_weight.shape[0])], kept)
    got, got_lse = to_x(kept), to_x(kept_lse)
    mine, unused = combine(kept, got, kept_lse, got_lse, mark)
    other = to_core(mine)

    terms = list(project(scalars, mine, other, out_held, tp_size))
    chunks = cut(gate_weight.shape[1])
    pair = [gate_weight.T, up_weight.T]
    (gate0, up0, gate1), mark, terms[1] = fetch(
        pair + pair[:1], [chunks[0], chunks[0], chunks[1]], terms[1]
    )
    passed = [to_z(terms[k], k) for k in (1, 3, 2)]
    h1 = add_residual(scalars, resid, terms[0], passed, mark)

    natural = g ^ jnp.arange(groups, dtype=jnp.int32)
    by_z = [h1, to_z(h1, 1), to_z(h1, 2)]
    across = None
    if groups == 2:
        by_z[2], across = lax.optimization_barrier((by_z[2], to_y(h1)))
    by_z.append(to_z(by_z[2], 1))
    (up1,), mark, by_z[1] = fetch(pair[1:], chunks[1:], by_z[1])
    held = [(gate0, up0), (gate1, up1)]
    sources = []
    for part in by_z:
        if groups == 2:
            sources += [part, to_y(part) if sources else across]
        else:
            everyone = jnp.take(lax.all_gather(part, "grp"), natural, axis=0)
            sources += [everyone[s] for s in range(groups)]
    scaled, squares = scale_rows(scalars, sources, gain[None, :], mark)

    first, second = (width for begin, width in chunks)
    keep0, cross, side, far_side = gate_up(scaled, *held[0], first, squares)
    cross = (cross.astype(F32) + to_core(far_side).astype(F32)).astype(BF16)
    got0 = to_core(side)
    scaled, cross = lax.optimization_barrier((scaled, cross))
    crossed0 = to_x(cross)
    keep1, cross, side, far_side = gate_up(scaled, *held[1], second)
    got, crossed0 = lax.optimization_barrier((to_core(far_side), crossed0))
    cross = (cross.astype(F32) + got.astype(F32)).astype(BF16)
    got1 = to_core(side)
    held, mark, cross = fetch([down_weight] * 2, chunks, cross)
    crossed1 = to_x(cross)
    hidden, norm = activate(model, first, keep0, got0, crossed0, None, mark)
    over, near = to_x(hidden), to_core(hidden)
    later, norm = activate(model, second, keep1, got1, crossed1, norm, hidden)
    far = to_x(later)
    over, later = lax.optimization_barrier((over, later))
    pieces = [hidden, over, near, to_core(over)]
    (total,) = down(scalars, pieces, held[0], None, groups, False)
    far, total = lax.optimization_barrier((far, total))
    pieces = [later, far, to_core(later), to_core(far)]
    result = down(scalars, pieces, held[1], total, groups, True)

    chunk_sums = []
    for k in range(4):
        own = result[k * groups]
        others = result[k * groups + 1 : (k + 1) * groups]
        if groups == 2:
            chunk_sums.append((own, others[0]))
        else:
            stacked = jnp.stack([own.astype(BF16)] + list(others))
            stacked = jnp.take(stacked, natural, axis=0)
            moved = lax.all_to_all(stacked, "grp", split_axis=0, concat_axis=0, tiled=True)
            chunk_sums.append(jnp.sum(moved.astype(F32), axis=0))
    parts = [h1]
    for k in (3, 2, 1, 0):
        if groups == 2:
            own, away = chunk_sums[k]
            away = to_y(away)
            if k == 0:
                parts += [own, away]
                continue
            value = own + away.astype(F32)
        else:
            value = chunk_sums[k]
        parts.append(value if k == 0 else to_z(value.astype(BF16), k))
    total = sum(part.astype(F32) for part in parts)
    live = t * rows + jnp.arange(rows, dtype=jnp.int32) < length
    return jnp.where(live[:, None], total, 0.0).astype(BF16)


def merged(x, axis, combine):
    everything = jax.tree.map(lambda part: lax.all_gather(part, axis), x)
    leading = jax.tree.map(lambda part: part[0], everything)

    def hop(k, so_far):
        return combine(so_far, jax.tree.map(lambda part: part[k], everything))

    return lax.fori_loop(1, lax.axis_size(axis), hop, leading)


def combine_parts(first, second):
    top = jnp.maximum(first[0], second[0])
    left = jnp.exp(first[0] - top)
    right = jnp.exp(second[0] - top)
    total = first[1] * left + second[1] * right
    values = first[2] * left[..., None] + second[2] * right[..., None]
    return (top, total, values)


def general_body(
    queries,
    new_kv,
    kv_cache,
    lengths,
    prefixes,
    resid,
    out_weight,
    gain,
    gate_weight,
    up_weight,
    down_weight,
):
    span, qcols = queries.shape
    kcols = new_kv.shape[2]
    local_kv = kcols // DH
    group = qcols // DH // local_kv
    cache_len = kv_cache.shape[2]
    length = lengths[0]
    model = gain.shape[0] * lax.axis_size("ffn")
    prefix = prefixes[0]
    width_index = lax.axis_index("ffn")
    shard_start = width_index * cache_len
    query_heads = (
        queries.reshape(span, local_kv, group, DH)
        .transpose(1, 2, 0, 3)
        .reshape(local_kv, group * span, DH)
    )
    row_pos = jnp.tile(jnp.arange(span, dtype=jnp.int32), group)
    inv_scale = 1.0 / math.sqrt(DH)

    def update(state, keys, values, valid):
        top, total, acc = state
        scores = (
            jnp.einsum("hrd,hkd->hrk", query_heads, keys, preferred_element_type=jnp.float32)
            * inv_scale
        )
        scores = jnp.where(valid[None], scores, NEGATIVE)
        new_top = jnp.maximum(top, jnp.max(scores, axis=-1))
        probs = jnp.where(valid[None], jnp.exp(scores - new_top[..., None]), 0.0)
        factor = jnp.exp(top - new_top)
        total = total * factor + jnp.sum(probs, axis=-1)
        acc = acc * factor[..., None] + jnp.einsum(
            "hrk,hkd->hrd", probs, values.astype(jnp.float32)
        )
        return (new_top, total, acc)

    block = math.gcd(512, cache_len)
    blocks = cache_len // block
    cache_keys = kv_cache[0, 0].reshape(blocks, block, local_kv, DH).transpose(0, 2, 1, 3)
    cache_values = kv_cache[1, 0].reshape(blocks, block, local_kv, DH).transpose(0, 2, 1, 3)
    rows = group * span
    start_state = (
        jnp.full((local_kv, rows), NEGATIVE, jnp.float32),
        jnp.zeros((local_kv, rows), jnp.float32),
        jnp.zeros((local_kv, rows, DH), jnp.float32),
    )

    def cache_step(state, items):
        keys, values, index = items
        positions = shard_start + index * block + jnp.arange(block, dtype=jnp.int32)
        valid = jnp.broadcast_to((positions < prefix)[None, :], (rows, block))
        return (update(state, keys, values, valid), None)

    state, unused = lax.scan(
        cache_step, start_state, (cache_keys, cache_values, jnp.arange(blocks, dtype=jnp.int32))
    )
    block_keys = new_kv[0].reshape(span, local_kv, DH).transpose(1, 0, 2)
    block_values = new_kv[1].reshape(span, local_kv, DH).transpose(1, 0, 2)
    slots = jnp.arange(span, dtype=jnp.int32)[None, :]
    new_valid = (slots < length) & (slots <= row_pos[:, None]) & (width_index == 0)
    state = update(state, block_keys, block_values, new_valid)
    top, total, acc = merged(state, "ffn", combine_parts)
    heads = acc / total[..., None]
    attn = (
        heads.reshape(local_kv, group, span, DH)
        .transpose(2, 0, 1, 3)
        .reshape(span, qcols)
        .astype(jnp.bfloat16)
    )
    partial_value = jnp.dot(attn, out_weight, preferred_element_type=jnp.float32)
    summed = lax.psum(partial_value, "tp")
    h1 = (summed + resid.astype(jnp.float32)).astype(jnp.bfloat16)
    all_rows = lax.all_gather(h1, "grp", axis=0, tiled=True)
    rows_f = all_rows.astype(jnp.float32)
    squares = jnp.sum(rows_f * rows_f, axis=1)
    scaled = (rows_f * gain.astype(jnp.float32)[None, :]).astype(jnp.bfloat16)
    gate = jnp.dot(scaled, gate_weight, preferred_element_type=jnp.float32)
    upper = jnp.dot(scaled, up_weight, preferred_element_type=jnp.float32)
    rows_here = span // lax.axis_size("tp")
    gate, upper, squares = lax.psum((gate, upper, squares), "ffn")
    inv_rms = lax.rsqrt(squares / model + 1e-06)
    hidden = (jax.nn.silu(gate * inv_rms[:, None]) * (upper * inv_rms[:, None])).astype(
        jnp.bfloat16
    )
    down_rows = lax.psum_scatter(
        jnp.dot(hidden, down_weight, preferred_element_type=jnp.float32),
        ("grp", "tp"),
        scatter_dimension=0,
        tiled=True,
    )
    row_start = lax.axis_index("tp") * rows_here
    own = lax.dynamic_slice_in_dim(h1, row_start, rows_here, 0)
    live = row_start + jnp.arange(rows_here, dtype=jnp.int32) < length
    return jnp.where(live[:, None], own.astype(jnp.float32) + down_rows, 0.0).astype(jnp.bfloat16)


def solution(mesh):
    sizes = tuple(mesh.shape[axis] for axis in ("grp", "tp", "ffn"))
    return jax.shard_map(
        body if sizes == (2, 4, 4) else general_body,
        mesh=mesh,
        in_specs=(
            P("grp", "tp"),
            P(None, "grp", "tp"),
            P(None, "grp", "ffn", "tp"),
            P("grp"),
            P("grp"),
            P("grp", "ffn"),
            P("tp", "ffn"),
            P("ffn"),
            P("ffn", ("grp", "tp")),
            P("ffn", ("grp", "tp")),
            P(("grp", "tp"), "ffn"),
        ),
        out_specs=P(("grp", "tp"), "ffn"),
        check_vma=False,
    )
```

```python
import functools
import math

import jax
import jax.numpy as jnp
from jax import lax
from jax.experimental import pallas as pl
from jax.experimental.pallas import tpu as pltpu
from jax.sharding import PartitionSpec as P

DH = 128
TILE = 1920
CHUNKS = (1, 1)
HEADS = 4
THIN = 1
NEGATIVE = -1e30
BF16 = jnp.bfloat16
F32 = jnp.float32
LIMIT = 8 * 1024 * 1024
ORDER = (0, 2, 1, 3)


def swapped_bits(index):
    return (index & 1) * 2 + (index >> 1)


def params(limit=LIMIT):
    return pltpu.CompilerParams(vmem_limit_bytes=limit)


def cost(flops, moved, exps=0):
    return pl.CostEstimate(
        flops=int(flops) // THIN, bytes_accessed=int(moved) // THIN, transcendentals=int(exps) // THIN
    )


def whole(shape):
    return pl.BlockSpec(shape, lambda *unused: (0,) * len(shape))


def fetch_kernel(pieces, *refs):
    count = len(pieces)
    sources, targets, mark, done = refs[:count], refs[count : 2 * count], refs[-2], refs[-1]
    copies = []
    for i, (begin, width) in enumerate(pieces):
        source = sources[i].at[pl.ds(begin, width)]
        copies.append(pltpu.make_async_copy(source, targets[i], done.at[i]))
    for copy in copies:
        copy.start()
    mark[...] = jnp.zeros_like(mark)
    for copy in copies:
        copy.wait()


def fetch(weights, pieces, after):
    *weights, after = lax.optimization_barrier((*weights, after))
    weights = [pltpu.with_memory_space_constraint(weight, pltpu.HBM) for weight in weights]
    shapes = [
        jax.ShapeDtypeStruct((width, weight.shape[1]), weight.dtype)
        for weight, (begin, width) in zip(weights, pieces)
    ]
    *held, mark = pl.pallas_call(
        functools.partial(fetch_kernel, pieces),
        in_specs=[pl.BlockSpec(memory_space=pltpu.HBM)] * len(weights),
        out_specs=[pl.BlockSpec(memory_space=pltpu.VMEM)] * (len(weights) + 1),
        out_shape=shapes + [jax.ShapeDtypeStruct((8, 128), F32)],
        scratch_shapes=[pltpu.SemaphoreType.DMA((len(weights),))],
        compiler_params=params(),
        cost_estimate=cost(0, 4 * sum(shape.size for shape in shapes)),
    )(*weights)
    return held, mark, after


def attention_kernel(
    scalars, q_ref, key_ref, value_ref, new_key_ref, new_value_ref, sent_ref, kept_ref, sent_lse_ref, kept_lse_ref, columns
):
    step = pl.program_id(0)
    span = q_ref.shape[0]
    cache_len = key_ref.shape[2]
    per_kv = sent_lse_ref.shape[0]
    usable, length, first = scalars[1], scalars[2], scalars[3]
    scale = 1.0 / math.sqrt(DH)
    position = lax.broadcasted_iota(jnp.int32, (1, cache_len), 1)
    bias = jnp.where(position < usable, 0.0, NEGATIVE)
    row = lax.broadcasted_iota(jnp.int32, (span, span), 0)
    col = lax.broadcasted_iota(jnp.int32, (span, span), 1)
    allowed = (col <= row) & (col < length) & (first > 0)
    fresh_bias = jnp.concatenate([jnp.where(allowed, 0.0, NEGATIVE)] * HEADS, axis=0)
    contract = (((1,), (1,)), ((), ()))
    keys, values = key_ref[0, 0], value_ref[0, 0]
    new_keys, new_values = new_key_ref[0], new_value_ref[0]
    columns[...] = jnp.zeros_like(columns)
    for low in range(0, per_kv, HEADS):
        heads = range(low, low + HEADS)
        q = jnp.concatenate([q_ref[:, h * DH : (h + 1) * DH] for h in heads], axis=0)
        scores = lax.dot_general(q, keys, contract, preferred_element_type=F32) * scale + bias
        fresh = lax.dot_general(q, new_keys, contract, preferred_element_type=F32)
        fresh = fresh * scale + fresh_bias
        top = jnp.maximum(
            jnp.max(scores, axis=1, keepdims=True), jnp.max(fresh, axis=1, keepdims=True)
        )
        probs = jnp.exp(scores - top)
        fresh_probs = jnp.exp(fresh - top)
        total = jnp.sum(probs, axis=1, keepdims=True) + jnp.sum(fresh_probs, axis=1, keepdims=True)
        mixed = jnp.dot(probs.astype(BF16), values, preferred_element_type=F32)
        mixed += jnp.dot(fresh_probs.astype(BF16), new_values, preferred_element_type=F32)
        mixed = (mixed / total).astype(BF16)
        lse = top + jnp.log(total)
        for i, h in enumerate(heads):
            columns[0:span, h : h + 1] = lse[i * span : (i + 1) * span]
            piece = mixed[i * span : (i + 1) * span]

            @pl.when(step == 0)
            def to_sent():
                sent_ref[:, h * DH : (h + 1) * DH] = piece

            @pl.when(step == 1)
            def to_kept():
                kept_ref[:, h * DH : (h + 1) * DH] = piece

    rows = jnp.transpose(columns[...])[0:per_kv, :]

    @pl.when(step == 0)
    def lse_sent():
        sent_lse_ref[...] = rows

    @pl.when(step == 1)
    def lse_kept():
        kept_lse_ref[...] = rows


def attention(scalars, queries, kv_cache, new_kv):
    span, qcols = queries.shape
    per_kv = qcols // DH // 2
    cache_len = kv_cache.shape[2]
    width = per_kv * DH

    def which(i, s):
        return s[0] ^ 1 ^ i

    def at_home(array):
        return pltpu.with_memory_space_constraint(array, pltpu.HBM)

    call = pl.pallas_call(
        attention_kernel,
        grid_spec=pltpu.PrefetchScalarGridSpec(
            num_scalar_prefetch=1,
            grid=(2,),
            in_specs=[
                pl.BlockSpec((span, width), lambda i, s: (0, which(i, s))),
                pl.BlockSpec((1, 1, cache_len, DH), lambda i, s: (0, 0, 0, which(i, s))),
                pl.BlockSpec((1, 1, cache_len, DH), lambda i, s: (1, 0, 0, which(i, s))),
                pl.BlockSpec((1, span, DH), lambda i, s: (0, 0, which(i, s))),
                pl.BlockSpec((1, span, DH), lambda i, s: (1, 0, which(i, s))),
            ],
            out_specs=[whole((span, width))] * 2 + [whole((per_kv, 128))] * 2,
            scratch_shapes=[pltpu.VMEM((128, 128), F32)],
        ),
        out_shape=[jax.ShapeDtypeStruct((span, width), BF16)] * 2
        + [jax.ShapeDtypeStruct((per_kv, 128), F32)] * 2,
        compiler_params=params(40 * 1024 * 1024),
        cost_estimate=cost(
            8 * span * per_kv * cache_len * DH, 8 * cache_len * DH, 2 * span * per_kv * cache_len
        ),
    )
    queries, kv_cache, new_kv = at_home(queries), at_home(kv_cache), at_home(new_kv)
    return call(scalars, queries, kv_cache, kv_cache, new_kv, new_kv)


def combine_kernel(last, a_ref, b_ref, lse_a_ref, lse_b_ref, *rest):
    out_ref = rest[-1] if last else rest[-2]
    span = a_ref.shape[0]
    heads = lse_a_ref.shape[0]
    lse_a, lse_b = lse_a_ref[...], lse_b_ref[...]
    top = jnp.maximum(lse_a, lse_b)
    left, right = jnp.exp(lse_a - top), jnp.exp(lse_b - top)
    total = left + right
    if not last:
        rest[-1][...] = top + jnp.log(total)
    pad = jnp.zeros((128 - 2 * heads, 128), F32)
    table = jnp.transpose(jnp.concatenate([left / total, right / total, pad], axis=0))
    for h in range(heads):
        cols = slice(h * DH, (h + 1) * DH)
        mixed = a_ref[:, cols].astype(F32) * table[0:span, h : h + 1]
        mixed += b_ref[:, cols].astype(F32) * table[0:span, heads + h : heads + h + 1]
        out_ref[:, cols] = mixed.astype(BF16)


def combine(a, b, lse_a, lse_b, last, *behind):
    shapes = [jax.ShapeDtypeStruct(a.shape, BF16)]
    if not last:
        shapes.append(jax.ShapeDtypeStruct(lse_a.shape, F32))
    return pl.pallas_call(
        functools.partial(combine_kernel, last),
        out_shape=shapes,
        compiler_params=params(),
        cost_estimate=cost(4 * a.size, 6 * a.size),
    )(a, b, lse_a, lse_b, *behind)


def project_kernel(scalars, keep_ref, other_ref, weight_ref, *rest):
    outs, acc = rest[:-1], rest[-1]
    step = pl.program_id(0)
    depth = weight_ref.shape[0]
    half = pl.num_programs(0) // 2
    rows = outs[0].shape[0]

    @pl.when(step < half)
    def from_keep():
        start = pl.multiple_of(step * depth, depth)
        term = jnp.dot(keep_ref[:, pl.ds(start, depth)], weight_ref[...], preferred_element_type=F32)

        @pl.when(step == 0)
        def begin():
            acc[...] = term

        @pl.when(step > 0)
        def go_on():
            acc[...] += term

    @pl.when(step >= half)
    def from_other():
        start = pl.multiple_of((step - half) * depth, depth)
        acc[...] += jnp.dot(
            other_ref[:, pl.ds(start, depth)], weight_ref[...], preferred_element_type=F32
        )

    @pl.when(step == pl.num_programs(0) - 1)
    def finish():
        for k, out in enumerate(outs):
            start = pl.multiple_of((scalars[4] ^ k) * rows, 8)
            out[...] = acc[pl.ds(start, rows), :].astype(out.dtype)


def project(scalars, keep, other, out_weight, tp_size):
    span, width = keep.shape
    depth = width
    half = width // depth
    cols = out_weight.shape[1]
    rows = span // tp_size
    return pl.pallas_call(
        project_kernel,
        grid_spec=pltpu.PrefetchScalarGridSpec(
            num_scalar_prefetch=1,
            grid=(2 * half,),
            in_specs=[
                whole((span, width)),
                whole((span, width)),
                pl.BlockSpec(
                    (depth, cols),
                    lambda i, s: (jnp.where(i < half, s[0], 1 - s[0]) * half + i % half, 0),
                ),
            ],
            out_specs=[whole((rows, cols))] * tp_size,
            scratch_shapes=[pltpu.VMEM((span, cols), F32)],
        ),
        out_shape=[
            jax.ShapeDtypeStruct((rows, cols), F32 if k == 0 else BF16) for k in range(tp_size)
        ],
        compiler_params=params(),
        cost_estimate=cost(4 * span * width * cols, 4 * width * cols),
    )(scalars, keep, other, out_weight)


def residual_kernel(scalars, resid_ref, first_ref, *rest):
    out_ref, spread = rest[-2:]
    rows = out_ref.shape[0]
    spread[...] = resid_ref[...].astype(F32)
    total = first_ref[...] + spread[pl.ds(pl.multiple_of(scalars[4] * rows, 8), rows), :]
    for term in rest[:3]:
        total += term[...].astype(F32)
    out_ref[...] = total.astype(BF16)


def add_residual(scalars, resid, first, others, *behind):
    shape = first.shape
    ins = [resid, first, *others, *behind]
    return pl.pallas_call(
        residual_kernel,
        grid_spec=pltpu.PrefetchScalarGridSpec(
            num_scalar_prefetch=1,
            grid=(1,),
            in_specs=[whole(part.shape) for part in ins],
            out_specs=whole(shape),
            scratch_shapes=[pltpu.VMEM(resid.shape, F32)],
        ),
        out_shape=jax.ShapeDtypeStruct(shape, BF16),
        compiler_params=params(),
        cost_estimate=cost(5 * first.size, 12 * first.size),
    )(scalars, *ins)


def scale_kernel(slots, scalars, *refs):
    count = 4 * slots
    sources, gain_ref = refs[:count], refs[count]
    scaled_ref, square_ref, ordered = refs[-3:]
    gain = gain_ref[...].astype(F32)
    cols = gain.shape[1]
    for k in range(4):
        place = swapped_bits(scalars[5] ^ k)
        rows = jnp.concatenate(
            [sources[k * slots + s][...].astype(F32) for s in range(slots)], axis=0
        )
        ordered[place] = rows * gain
        squares = rows * rows
        part = squares[:, 0:128]
        for c in range(128, cols, 128):
            part += squares[:, c : c + 128]
        square_ref[place] = part
    tall = ordered[...].reshape(scaled_ref.shape[1], cols)
    scaled_ref[...] = jnp.transpose(tall).astype(BF16)


def scale_rows(scalars, sources, gain, mark):
    slots = len(sources) // 4
    rows, cols = sources[0].shape
    high = rows * slots
    return pl.pallas_call(
        functools.partial(scale_kernel, slots),
        grid_spec=pltpu.PrefetchScalarGridSpec(
            num_scalar_prefetch=1,
            grid=(1,),
            in_specs=[whole((rows, cols))] * len(sources) + [whole((1, cols)), whole(mark.shape)],
            out_specs=[whole((cols, 4 * high)), whole((4, high, 128))],
            scratch_shapes=[pltpu.VMEM((4, high, cols), F32)],
        ),
        out_shape=[
            jax.ShapeDtypeStruct((cols, 4 * high), BF16),
            jax.ShapeDtypeStruct((4, high, 128), F32),
        ],
        compiler_params=params(),
        cost_estimate=cost(4 * 4 * high * cols, 4 * 4 * high * cols),
    )(scalars, *sources, gain, mark)


def gate_up_kernel(scaled_ref, gate_ref, up_ref, *rest):
    homes = rest[-4:]
    high = homes[0].shape[1]
    width = gate_ref.shape[0]
    for which, weight in enumerate((gate_ref, up_ref)):
        term = jnp.dot(weight[...], scaled_ref[...], preferred_element_type=F32)
        term = jnp.transpose(term).astype(BF16)
        for place, home in enumerate(homes):
            home[which, :, 0:width] = term[place * high : (place + 1) * high]
    if len(rest) > 4:
        for place, home in enumerate(homes):
            home[0, :, width:] = rest[0][place].astype(BF16)
            home[1, :, width:] = jnp.zeros((high, 128), BF16)


def gate_up(scaled, gate_weight, up_weight, width, squares=None):
    depth, rows = scaled.shape
    high = rows // 4
    flops, moved = 4 * rows * depth * width, 4 * depth * width
    ins = [scaled, gate_weight, up_weight]
    if squares is not None:
        ins.append(squares)
        width += 128
    return pl.pallas_call(
        gate_up_kernel,
        out_shape=[jax.ShapeDtypeStruct((2, high, width), BF16)] * 4,
        compiler_params=params(),
        cost_estimate=cost(flops, moved),
    )(*ins)


def activate_kernel(model, width, own_norm, keep_ref, got_ref, crossed_ref, *rest):
    def total(which, low, high):
        value = keep_ref[which, :, low:high].astype(F32)
        value += got_ref[which, :, low:high].astype(F32)
        return value + crossed_ref[which, :, low:high].astype(F32)

    if own_norm:
        hidden_ref, norm_ref = rest[-2:]
        squares = jnp.sum(total(0, width, width + 128), axis=1, keepdims=True)
        norm = lax.rsqrt(squares / model + 1e-06)
        norm_ref[...] = jnp.broadcast_to(norm, norm_ref.shape)
    else:
        hidden_ref = rest[-1]
        norm = rest[0][:, 0:1]
    gate = total(0, 0, width) * norm
    up = total(1, 0, width) * norm
    hidden_ref[...] = (gate / (1.0 + jnp.exp(-gate)) * up).astype(BF16)


def activate(model, width, keep, got, crossed, norm, *behind):
    high = keep.shape[1]
    shapes = [jax.ShapeDtypeStruct((high, width), BF16)]
    if norm is None:
        shapes.append(jax.ShapeDtypeStruct((high, 128), F32))
    ins = [keep, got, crossed] + ([] if norm is None else [norm]) + list(behind)
    result = pl.pallas_call(
        functools.partial(activate_kernel, model, width, norm is None),
        out_shape=shapes,
        compiler_params=params(),
        cost_estimate=cost(20 * high * width, 14 * high * width, high * width),
    )(*ins)
    return result if norm is None else (result[0], norm)


def down_kernel(width, slots, has_start, last, scalars, *refs):
    hidden = refs[0:4]
    weight_ref = refs[4]
    rest = list(refs[5:])
    start_ref = rest.pop(0) if has_start else None
    acc, packed = rest[-2], rest[-1]
    outs = rest[:-2]
    step = pl.program_id(0)
    depth = weight_ref.shape[0]
    high = hidden[0].shape[0]
    steps = pl.num_programs(0)

    @pl.when(step == 0)
    def begin():
        if width % depth:
            packed[...] = jnp.zeros_like(packed)
        for place in range(4):
            packed[place * high : (place + 1) * high, 0:width] = hidden[place][...]
        if has_start:
            acc[...] = start_ref[...]
        else:
            acc[...] = jnp.zeros_like(acc)

    def add(weight):
        if packed.shape[1] == depth:
            part = packed[...]
        else:
            part = packed[:, pl.ds(pl.multiple_of(step * depth, depth), depth)]
        term = jnp.dot(part, weight, preferred_element_type=F32)
        acc[...] += term.reshape(acc.shape)

    if width % depth:

        @pl.when(step < steps - 1)
        def inner():
            add(weight_ref[...])

        @pl.when(step == steps - 1)
        def edge():
            row = lax.broadcasted_iota(jnp.int32, weight_ref.shape, 0)
            add(jnp.where(row < width % depth, weight_ref[...], jnp.zeros_like(weight_ref)))
    else:
        add(weight_ref[...])

    @pl.when(step == steps - 1)
    def finish():
        if not last:
            outs[0][...] = acc[...]
            return
        rows = high // slots
        for k in range(4):
            place = swapped_bits(scalars[5] ^ k)
            block = acc[place]
            for s in range(slots):
                out = outs[k * slots + s]
                out[...] = block[s * rows : (s + 1) * rows].astype(out.dtype)


def down(scalars, hidden, down_weight, start, slots, last):
    high, width = hidden[0].shape
    cols = down_weight.shape[1]
    tile = min(TILE, width)
    steps = pl.cdiv(width, tile)
    rows = high // slots
    ins = [whole((high, width))] * 4 + [pl.BlockSpec((tile, cols), lambda i, s: (i, 0))]
    args = list(hidden) + [down_weight]
    if start is not None:
        ins.append(whole((4, high, cols)))
        args.append(start)
    if last:
        shapes = [
            jax.ShapeDtypeStruct((rows, cols), F32 if s == 0 else BF16)
            for k in range(4)
            for s in range(slots)
        ]
    else:
        shapes = [jax.ShapeDtypeStruct((4, high, cols), F32)]
    return pl.pallas_call(
        functools.partial(down_kernel, width, slots, start is not None, last),
        grid_spec=pltpu.PrefetchScalarGridSpec(
            num_scalar_prefetch=1,
            grid=(steps,),
            in_specs=ins,
            out_specs=[whole(shape.shape) for shape in shapes],
            scratch_shapes=[
                pltpu.VMEM((4, high, cols), F32),
                pltpu.VMEM((4 * high, steps * tile), BF16),
            ],
        ),
        out_shape=shapes,
        compiler_params=params(),
        cost_estimate=cost(8 * high * width * cols, 2 * width * cols),
    )(scalars, *args)


def to_core(x):
    return lax.ppermute(x, "ffn", [(i, i ^ 1) for i in range(4)])


def to_x(x):
    return lax.ppermute(x, "ffn", [(i, i ^ 2) for i in range(4)])


def to_z(x, k):
    return lax.ppermute(x, "tp", [(i, i ^ k) for i in range(4)])


def to_y(x):
    return lax.ppermute(x, "grp", [(0, 1), (1, 0)])


def cut(total):
    edges = [0]
    for tiles in CHUNKS:
        edges.append(min(edges[-1] + tiles * TILE, total))
    return [(low, high - low) for low, high in zip(edges, edges[1:])]


def body(
    queries,
    new_kv,
    kv_cache,
    lengths,
    prefixes,
    resid,
    out_weight,
    gain,
    gate_weight,
    up_weight,
    down_weight,
):
    span = queries.shape[0]
    local_kv = new_kv.shape[2] // DH
    cache_len = kv_cache.shape[2]
    groups = lax.axis_size("grp")
    tp_size = lax.axis_size("tp")
    g, t, f = lax.axis_index("grp"), lax.axis_index("tp"), lax.axis_index("ffn")
    core = f & 1
    length = lengths[0]
    rows = span // tp_size
    model = gain.shape[0] * lax.axis_size("ffn")
    usable = jnp.clip(prefixes[0] - f * cache_len, 0, cache_len)
    first = (f == 0).astype(jnp.int32)
    scalars = jnp.stack([core, usable, length, first, t, t ^ f]).astype(jnp.int32)
    scalars = lax.optimization_barrier(scalars)
    sent, kept, sent_lse, kept_lse = attention(scalars, queries, kv_cache, new_kv)
    got, got_lse = to_core(sent), to_core(sent_lse)
    kept, kept_lse = combine(kept, got, kept_lse, got_lse, False)
    (out_held,), mark, kept = fetch([out_weight], [(0, out_weight.shape[0])], kept)
    got, got_lse = to_x(kept), to_x(kept_lse)
    (mine,) = combine(kept, got, kept_lse, got_lse, True, mark)
    other = to_core(mine)

    terms = list(project(scalars, mine, other, out_held, tp_size))
    chunks = cut(gate_weight.shape[1])
    pair = [gate_weight.T, up_weight.T]
    (gate0, up0, gate1), mark, terms[1] = fetch(
        pair + pair[:1], [chunks[0], chunks[0], chunks[1]], terms[1]
    )
    passed = [to_z(terms[k], k) for k in (1, 3, 2)]
    h1 = add_residual(scalars, resid, terms[0], passed, mark)

    natural = g ^ jnp.arange(groups, dtype=jnp.int32)
    by_z = [h1, to_z(h1, 1), to_z(h1, 2)]
    across = None
    if groups == 2:
        by_z[2], across = lax.optimization_barrier((by_z[2], to_y(h1)))
    by_z.append(to_z(by_z[2], 1))
    (up1,), mark, by_z[1] = fetch(pair[1:], chunks[1:], by_z[1])
    held = [(gate0, up0), (gate1, up1)]
    sources = []
    for part in by_z:
        if groups == 2:
            sources += [part, to_y(part) if sources else across]
        else:
            everyone = jnp.take(lax.all_gather(part, "grp"), natural, axis=0)
            sources += [everyone[s] for s in range(groups)]
    scaled, squares = scale_rows(scalars, sources, gain[None, :], mark)

    first, second = (width for begin, width in chunks)
    keep0, cross, side, far_side = gate_up(scaled, *held[0], first, squares)
    cross = (cross.astype(F32) + to_core(far_side).astype(F32)).astype(BF16)
    got0 = to_core(side)
    scaled, cross = lax.optimization_barrier((scaled, cross))
    crossed0 = to_x(cross)
    keep1, cross, side, far_side = gate_up(scaled, *held[1], second)
    got, crossed0 = lax.optimization_barrier((to_core(far_side), crossed0))
    cross = (cross.astype(F32) + got.astype(F32)).astype(BF16)
    got1 = to_core(side)
    held, mark, cross = fetch([down_weight] * 2, chunks, cross)
    crossed1 = to_x(cross)
    hidden, norm = activate(model, first, keep0, got0, crossed0, None, mark)
    over, near = to_x(hidden), to_core(hidden)
    later, norm = activate(model, second, keep1, got1, crossed1, norm, hidden)
    far = to_x(later)
    over, later = lax.optimization_barrier((over, later))
    pieces = [hidden, over, near, to_core(over)]
    (total,) = down(scalars, pieces, held[0], None, groups, False)
    far, total = lax.optimization_barrier((far, total))
    pieces = [later, far, to_core(later), to_core(far)]
    result = down(scalars, pieces, held[1], total, groups, True)

    chunk_sums = []
    for k in range(4):
        own = result[k * groups]
        others = result[k * groups + 1 : (k + 1) * groups]
        if groups == 2:
            chunk_sums.append((own, others[0]))
        else:
            stacked = jnp.stack([own.astype(BF16)] + list(others))
            stacked = jnp.take(stacked, natural, axis=0)
            moved = lax.all_to_all(stacked, "grp", split_axis=0, concat_axis=0, tiled=True)
            chunk_sums.append(jnp.sum(moved.astype(F32), axis=0))
    parts = [h1]
    for k in (3, 2, 1, 0):
        if groups == 2:
            own, away = chunk_sums[k]
            away = to_y(away)
            if k == 0:
                parts += [own, away]
                continue
            value = own + away.astype(F32)
        else:
            value = chunk_sums[k]
        parts.append(value if k == 0 else to_z(value.astype(BF16), k))
    total = sum(part.astype(F32) for part in parts)
    live = t * rows + jnp.arange(rows, dtype=jnp.int32) < length
    return jnp.where(live[:, None], total, 0.0).astype(BF16)


def merged(x, axis, combine):
    everything = jax.tree.map(lambda part: lax.all_gather(part, axis), x)
    leading = jax.tree.map(lambda part: part[0], everything)

    def hop(k, so_far):
        return combine(so_far, jax.tree.map(lambda part: part[k], everything))

    return lax.fori_loop(1, lax.axis_size(axis), hop, leading)


def combine_parts(first, second):
    top = jnp.maximum(first[0], second[0])
    left = jnp.exp(first[0] - top)
    right = jnp.exp(second[0] - top)
    total = first[1] * left + second[1] * right
    values = first[2] * left[..., None] + second[2] * right[..., None]
    return (top, total, values)


def general_body(
    queries,
    new_kv,
    kv_cache,
    lengths,
    prefixes,
    resid,
    out_weight,
    gain,
    gate_weight,
    up_weight,
    down_weight,
):
    span, qcols = queries.shape
    kcols = new_kv.shape[2]
    local_kv = kcols // DH
    group = qcols // DH // local_kv
    cache_len = kv_cache.shape[2]
    length = lengths[0]
    model = gain.shape[0] * lax.axis_size("ffn")
    prefix = prefixes[0]
    width_index = lax.axis_index("ffn")
    shard_start = width_index * cache_len
    query_heads = (
        queries.reshape(span, local_kv, group, DH)
        .transpose(1, 2, 0, 3)
        .reshape(local_kv, group * span, DH)
    )
    row_pos = jnp.tile(jnp.arange(span, dtype=jnp.int32), group)
    inv_scale = 1.0 / math.sqrt(DH)

    def update(state, keys, values, valid):
        top, total, acc = state
        scores = (
            jnp.einsum("hrd,hkd->hrk", query_heads, keys, preferred_element_type=jnp.float32)
            * inv_scale
        )
        scores = jnp.where(valid[None], scores, NEGATIVE)
        new_top = jnp.maximum(top, jnp.max(scores, axis=-1))
        probs = jnp.where(valid[None], jnp.exp(scores - new_top[..., None]), 0.0)
        factor = jnp.exp(top - new_top)
        total = total * factor + jnp.sum(probs, axis=-1)
        acc = acc * factor[..., None] + jnp.einsum(
            "hrk,hkd->hrd", probs, values.astype(jnp.float32)
        )
        return (new_top, total, acc)

    block = math.gcd(512, cache_len)
    blocks = cache_len // block
    cache_keys = kv_cache[0, 0].reshape(blocks, block, local_kv, DH).transpose(0, 2, 1, 3)
    cache_values = kv_cache[1, 0].reshape(blocks, block, local_kv, DH).transpose(0, 2, 1, 3)
    rows = group * span
    start_state = (
        jnp.full((local_kv, rows), NEGATIVE, jnp.float32),
        jnp.zeros((local_kv, rows), jnp.float32),
        jnp.zeros((local_kv, rows, DH), jnp.float32),
    )

    def cache_step(state, items):
        keys, values, index = items
        positions = shard_start + index * block + jnp.arange(block, dtype=jnp.int32)
        valid = jnp.broadcast_to((positions < prefix)[None, :], (rows, block))
        return (update(state, keys, values, valid), None)

    state, unused = lax.scan(
        cache_step, start_state, (cache_keys, cache_values, jnp.arange(blocks, dtype=jnp.int32))
    )
    block_keys = new_kv[0].reshape(span, local_kv, DH).transpose(1, 0, 2)
    block_values = new_kv[1].reshape(span, local_kv, DH).transpose(1, 0, 2)
    slots = jnp.arange(span, dtype=jnp.int32)[None, :]
    new_valid = (slots < length) & (slots <= row_pos[:, None]) & (width_index == 0)
    state = update(state, block_keys, block_values, new_valid)
    top, total, acc = merged(state, "ffn", combine_parts)
    heads = acc / total[..., None]
    attn = (
        heads.reshape(local_kv, group, span, DH)
        .transpose(2, 0, 1, 3)
        .reshape(span, qcols)
        .astype(jnp.bfloat16)
    )
    partial_value = jnp.dot(attn, out_weight, preferred_element_type=jnp.float32)
    summed = lax.psum(partial_value, "tp")
    h1 = (summed + resid.astype(jnp.float32)).astype(jnp.bfloat16)
    all_rows = lax.all_gather(h1, "grp", axis=0, tiled=True)
    rows_f = all_rows.astype(jnp.float32)
    squares = jnp.sum(rows_f * rows_f, axis=1)
    scaled = (rows_f * gain.astype(jnp.float32)[None, :]).astype(jnp.bfloat16)
    gate = jnp.dot(scaled, gate_weight, preferred_element_type=jnp.float32)
    upper = jnp.dot(scaled, up_weight, preferred_element_type=jnp.float32)
    rows_here = span // lax.axis_size("tp")
    gate, upper, squares = lax.psum((gate, upper, squares), "ffn")
    inv_rms = lax.rsqrt(squares / model + 1e-06)
    hidden = (jax.nn.silu(gate * inv_rms[:, None]) * (upper * inv_rms[:, None])).astype(
        jnp.bfloat16
    )
    down_rows = lax.psum_scatter(
        jnp.dot(hidden, down_weight, preferred_element_type=jnp.float32),
        ("grp", "tp"),
        scatter_dimension=0,
        tiled=True,
    )
    row_start = lax.axis_index("tp") * rows_here
    own = lax.dynamic_slice_in_dim(h1, row_start, rows_here, 0)
    live = row_start + jnp.arange(rows_here, dtype=jnp.int32) < length
    return jnp.where(live[:, None], own.astype(jnp.float32) + down_rows, 0.0).astype(jnp.bfloat16)


def solution(mesh):
    sizes = tuple(mesh.shape[axis] for axis in ("grp", "tp", "ffn"))
    return jax.shard_map(
        body if sizes == (2, 4, 4) else general_body,
        mesh=mesh,
        in_specs=(
            P("grp", "tp"),
            P(None, "grp", "tp"),
            P(None, "grp", "ffn", "tp"),
            P("grp"),
            P("grp"),
            P("grp", "ffn"),
            P("tp", "ffn"),
            P("ffn"),
            P("ffn", ("grp", "tp")),
            P("ffn", ("grp", "tp")),
            P(("grp", "tp"), "ffn"),
        ),
        out_specs=P(("grp", "tp"), "ffn"),
        check_vma=False,
    )
```

```python
import functools
import math

import jax
import jax.numpy as jnp
from jax import lax
from jax.experimental import pallas as pl
from jax.experimental.pallas import tpu as pltpu
from jax.sharding import PartitionSpec as P

DH = 128
SPLIT = 1792
HEADS = 4
THIN = 1
NEGATIVE = -1e30
BF16 = jnp.bfloat16
F32 = jnp.float32
LIMIT = 8 * 1024 * 1024
ORDER = (0, 2, 1, 3)


def swapped_bits(index):
    return (index & 1) * 2 + (index >> 1)


def params(limit=LIMIT):
    return pltpu.CompilerParams(vmem_limit_bytes=limit)


def cost(flops, moved, exps=0):
    return pl.CostEstimate(
        flops=int(flops) // THIN, bytes_accessed=int(moved) // THIN, transcendentals=int(exps) // THIN
    )


def whole(shape):
    return pl.BlockSpec(shape, lambda *unused: (0,) * len(shape))


def fetch_kernel(pieces, *refs):
    count = len(pieces)
    sources, targets, mark, done = refs[:count], refs[count : 2 * count], refs[-2], refs[-1]
    copies = []
    for i, (begin, width) in enumerate(pieces):
        source = sources[i].at[pl.ds(begin, width)]
        copies.append(pltpu.make_async_copy(source, targets[i], done.at[i]))
    for copy in copies:
        copy.start()
    mark[...] = jnp.zeros_like(mark)
    for copy in copies:
        copy.wait()


def fetch(weights, pieces, after):
    *weights, after = lax.optimization_barrier((*weights, after))
    weights = [pltpu.with_memory_space_constraint(weight, pltpu.HBM) for weight in weights]
    shapes = [
        jax.ShapeDtypeStruct((width, weight.shape[1]), weight.dtype)
        for weight, (begin, width) in zip(weights, pieces)
    ]
    *held, mark = pl.pallas_call(
        functools.partial(fetch_kernel, pieces),
        in_specs=[pl.BlockSpec(memory_space=pltpu.HBM)] * len(weights),
        out_specs=[pl.BlockSpec(memory_space=pltpu.VMEM)] * (len(weights) + 1),
        out_shape=shapes + [jax.ShapeDtypeStruct((8, 128), F32)],
        scratch_shapes=[pltpu.SemaphoreType.DMA((len(weights),))],
        compiler_params=params(),
        cost_estimate=cost(0, 4 * sum(shape.size for shape in shapes)),
    )(*weights)
    return held, mark, after


def attention_kernel(
    scalars, q_ref, key_ref, value_ref, new_key_ref, new_value_ref, sent_ref, kept_ref, sent_lse_ref, kept_lse_ref, columns
):
    step = pl.program_id(0)
    span = q_ref.shape[0]
    cache_len = key_ref.shape[2]
    per_kv = sent_lse_ref.shape[0]
    usable, length, first = scalars[1], scalars[2], scalars[3]
    scale = 1.0 / math.sqrt(DH)
    position = lax.broadcasted_iota(jnp.int32, (1, cache_len), 1)
    bias = jnp.where(position < usable, 0.0, NEGATIVE)
    row = lax.broadcasted_iota(jnp.int32, (span, span), 0)
    col = lax.broadcasted_iota(jnp.int32, (span, span), 1)
    allowed = (col <= row) & (col < length) & (first > 0)
    fresh_bias = jnp.concatenate([jnp.where(allowed, 0.0, NEGATIVE)] * HEADS, axis=0)
    contract = (((1,), (1,)), ((), ()))
    keys, values = key_ref[0, 0], value_ref[0, 0]
    new_keys, new_values = new_key_ref[0], new_value_ref[0]
    columns[...] = jnp.zeros_like(columns)
    for low in range(0, per_kv, HEADS):
        heads = range(low, low + HEADS)
        q = jnp.concatenate([q_ref[:, h * DH : (h + 1) * DH] for h in heads], axis=0)
        scores = lax.dot_general(q, keys, contract, preferred_element_type=F32) * scale + bias
        fresh = lax.dot_general(q, new_keys, contract, preferred_element_type=F32)
        fresh = fresh * scale + fresh_bias
        top = jnp.maximum(
            jnp.max(scores, axis=1, keepdims=True), jnp.max(fresh, axis=1, keepdims=True)
        )
        probs = jnp.exp(scores - top)
        fresh_probs = jnp.exp(fresh - top)
        total = jnp.sum(probs, axis=1, keepdims=True) + jnp.sum(fresh_probs, axis=1, keepdims=True)
        mixed = jnp.dot(probs.astype(BF16), values, preferred_element_type=F32)
        mixed += jnp.dot(fresh_probs.astype(BF16), new_values, preferred_element_type=F32)
        mixed = (mixed / total).astype(BF16)
        lse = top + jnp.log(total)
        for i, h in enumerate(heads):
            columns[0:span, h : h + 1] = lse[i * span : (i + 1) * span]
            piece = mixed[i * span : (i + 1) * span]

            @pl.when(step == 0)
            def to_sent():
                sent_ref[:, h * DH : (h + 1) * DH] = piece

            @pl.when(step == 1)
            def to_kept():
                kept_ref[:, h * DH : (h + 1) * DH] = piece

    rows = jnp.transpose(columns[...])[0:per_kv, :]

    @pl.when(step == 0)
    def lse_sent():
        sent_lse_ref[...] = rows

    @pl.when(step == 1)
    def lse_kept():
        kept_lse_ref[...] = rows


def attention(scalars, queries, kv_cache, new_kv):
    span, qcols = queries.shape
    per_kv = qcols // DH // 2
    cache_len = kv_cache.shape[2]
    width = per_kv * DH

    def which(i, s):
        return s[0] ^ 1 ^ i

    def at_home(array):
        return pltpu.with_memory_space_constraint(array, pltpu.HBM)

    call = pl.pallas_call(
        attention_kernel,
        grid_spec=pltpu.PrefetchScalarGridSpec(
            num_scalar_prefetch=1,
            grid=(2,),
            in_specs=[
                pl.BlockSpec((span, width), lambda i, s: (0, which(i, s))),
                pl.BlockSpec((1, 1, cache_len, DH), lambda i, s: (0, 0, 0, which(i, s))),
                pl.BlockSpec((1, 1, cache_len, DH), lambda i, s: (1, 0, 0, which(i, s))),
                pl.BlockSpec((1, span, DH), lambda i, s: (0, 0, which(i, s))),
                pl.BlockSpec((1, span, DH), lambda i, s: (1, 0, which(i, s))),
            ],
            out_specs=[whole((span, width))] * 2 + [whole((per_kv, 128))] * 2,
            scratch_shapes=[pltpu.VMEM((128, 128), F32)],
        ),
        out_shape=[jax.ShapeDtypeStruct((span, width), BF16)] * 2
        + [jax.ShapeDtypeStruct((per_kv, 128), F32)] * 2,
        compiler_params=params(40 * 1024 * 1024),
        cost_estimate=cost(
            8 * span * per_kv * cache_len * DH, 8 * cache_len * DH, 2 * span * per_kv * cache_len
        ),
    )
    queries, kv_cache, new_kv = at_home(queries), at_home(kv_cache), at_home(new_kv)
    return call(scalars, queries, kv_cache, kv_cache, new_kv, new_kv)


def combine_kernel(last, a_ref, b_ref, lse_a_ref, lse_b_ref, *rest):
    out_ref = rest[-1] if last else rest[-2]
    span = a_ref.shape[0]
    heads = lse_a_ref.shape[0]
    lse_a, lse_b = lse_a_ref[...], lse_b_ref[...]
    top = jnp.maximum(lse_a, lse_b)
    left, right = jnp.exp(lse_a - top), jnp.exp(lse_b - top)
    total = left + right
    if not last:
        rest[-1][...] = top + jnp.log(total)
    pad = jnp.zeros((128 - 2 * heads, 128), F32)
    table = jnp.transpose(jnp.concatenate([left / total, right / total, pad], axis=0))
    for h in range(heads):
        cols = slice(h * DH, (h + 1) * DH)
        mixed = a_ref[:, cols].astype(F32) * table[0:span, h : h + 1]
        mixed += b_ref[:, cols].astype(F32) * table[0:span, heads + h : heads + h + 1]
        out_ref[:, cols] = mixed.astype(BF16)


def combine(a, b, lse_a, lse_b, last, *behind):
    shapes = [jax.ShapeDtypeStruct(a.shape, BF16)]
    if not last:
        shapes.append(jax.ShapeDtypeStruct(lse_a.shape, F32))
    return pl.pallas_call(
        functools.partial(combine_kernel, last),
        out_shape=shapes,
        compiler_params=params(),
        cost_estimate=cost(4 * a.size, 6 * a.size),
    )(a, b, lse_a, lse_b, *behind)


def project_kernel(scalars, keep_ref, other_ref, weight_ref, *rest):
    outs, acc = rest[:-1], rest[-1]
    step = pl.program_id(0)
    depth = weight_ref.shape[0]
    half = pl.num_programs(0) // 2
    rows = outs[0].shape[0]

    @pl.when(step < half)
    def from_keep():
        start = pl.multiple_of(step * depth, depth)
        term = jnp.dot(keep_ref[:, pl.ds(start, depth)], weight_ref[...], preferred_element_type=F32)

        @pl.when(step == 0)
        def begin():
            acc[...] = term

        @pl.when(step > 0)
        def go_on():
            acc[...] += term

    @pl.when(step >= half)
    def from_other():
        start = pl.multiple_of((step - half) * depth, depth)
        acc[...] += jnp.dot(
            other_ref[:, pl.ds(start, depth)], weight_ref[...], preferred_element_type=F32
        )

    @pl.when(step == pl.num_programs(0) - 1)
    def finish():
        for k, out in enumerate(outs):
            start = pl.multiple_of((scalars[4] ^ k) * rows, 8)
            out[...] = acc[pl.ds(start, rows), :].astype(out.dtype)


def project(scalars, keep, other, out_weight, tp_size):
    span, width = keep.shape
    depth = width
    half = width // depth
    cols = out_weight.shape[1]
    rows = span // tp_size
    return pl.pallas_call(
        project_kernel,
        grid_spec=pltpu.PrefetchScalarGridSpec(
            num_scalar_prefetch=1,
            grid=(2 * half,),
            in_specs=[
                whole((span, width)),
                whole((span, width)),
                pl.BlockSpec(
                    (depth, cols),
                    lambda i, s: (jnp.where(i < half, s[0], 1 - s[0]) * half + i % half, 0),
                ),
            ],
            out_specs=[whole((rows, cols))] * tp_size,
            scratch_shapes=[pltpu.VMEM((span, cols), F32)],
        ),
        out_shape=[
            jax.ShapeDtypeStruct((rows, cols), F32 if k == 0 else BF16) for k in range(tp_size)
        ],
        compiler_params=params(),
        cost_estimate=cost(4 * span * width * cols, 4 * width * cols),
    )(scalars, keep, other, out_weight)


def residual_kernel(scalars, resid_ref, first_ref, *rest):
    out_ref, spread = rest[-2:]
    rows = out_ref.shape[0]
    spread[...] = resid_ref[...].astype(F32)
    total = first_ref[...] + spread[pl.ds(pl.multiple_of(scalars[4] * rows, 8), rows), :]
    for term in rest[:3]:
        total += term[...].astype(F32)
    out_ref[...] = total.astype(BF16)


def add_residual(scalars, resid, first, others, *behind):
    shape = first.shape
    ins = [resid, first, *others, *behind]
    return pl.pallas_call(
        residual_kernel,
        grid_spec=pltpu.PrefetchScalarGridSpec(
            num_scalar_prefetch=1,
            grid=(1,),
            in_specs=[whole(part.shape) for part in ins],
            out_specs=whole(shape),
            scratch_shapes=[pltpu.VMEM(resid.shape, F32)],
        ),
        out_shape=jax.ShapeDtypeStruct(shape, BF16),
        compiler_params=params(),
        cost_estimate=cost(5 * first.size, 12 * first.size),
    )(scalars, *ins)


def scale_kernel(slots, scalars, *refs):
    count = 4 * slots
    sources, gain_ref = refs[:count], refs[count]
    scaled_ref, square_ref, ordered = refs[-3:]
    gain = gain_ref[...].astype(F32)
    cols = gain.shape[1]
    for k in range(4):
        place = swapped_bits(scalars[5] ^ k)
        rows = jnp.concatenate(
            [sources[k * slots + s][...].astype(F32) for s in range(slots)], axis=0
        )
        ordered[place] = rows * gain
        squares = rows * rows
        part = squares[:, 0:128]
        for c in range(128, cols, 128):
            part += squares[:, c : c + 128]
        square_ref[place] = part
    tall = ordered[...].reshape(scaled_ref.shape[1], cols)
    scaled_ref[...] = jnp.transpose(tall).astype(BF16)


def scale_rows(scalars, sources, gain, mark):
    slots = len(sources) // 4
    rows, cols = sources[0].shape
    high = rows * slots
    return pl.pallas_call(
        functools.partial(scale_kernel, slots),
        grid_spec=pltpu.PrefetchScalarGridSpec(
            num_scalar_prefetch=1,
            grid=(1,),
            in_specs=[whole((rows, cols))] * len(sources) + [whole((1, cols)), whole(mark.shape)],
            out_specs=[whole((cols, 4 * high)), whole((4, high, 128))],
            scratch_shapes=[pltpu.VMEM((4, high, cols), F32)],
        ),
        out_shape=[
            jax.ShapeDtypeStruct((cols, 4 * high), BF16),
            jax.ShapeDtypeStruct((4, high, 128), F32),
        ],
        compiler_params=params(),
        cost_estimate=cost(4 * 4 * high * cols, 4 * 4 * high * cols),
    )(scalars, *sources, gain, mark)


def gate_up_kernel(scaled_ref, gate_ref, up_ref, *rest):
    homes = rest[-4:]
    high = homes[0].shape[1]
    width = gate_ref.shape[0]
    for which, weight in enumerate((gate_ref, up_ref)):
        term = jnp.dot(weight[...], scaled_ref[...], preferred_element_type=F32)
        term = jnp.transpose(term).astype(BF16)
        for place, home in enumerate(homes):
            home[which, :, 0:width] = term[place * high : (place + 1) * high]
    if len(rest) > 4:
        for place, home in enumerate(homes):
            home[0, :, width:] = rest[0][place].astype(BF16)
            home[1, :, width:] = jnp.zeros((high, 128), BF16)


def gate_up(scaled, gate_weight, up_weight, width, squares=None):
    depth, rows = scaled.shape
    high = rows // 4
    flops, moved = 4 * rows * depth * width, 4 * depth * width
    ins = [scaled, gate_weight, up_weight]
    if squares is not None:
        ins.append(squares)
        width += 128
    return pl.pallas_call(
        gate_up_kernel,
        out_shape=[jax.ShapeDtypeStruct((2, high, width), BF16)] * 4,
        compiler_params=params(),
        cost_estimate=cost(flops, moved),
    )(*ins)


def activate_kernel(model, width, own_norm, keep_ref, got_ref, crossed_ref, *rest):
    def total(which, low, high):
        value = keep_ref[which, :, low:high].astype(F32)
        value += got_ref[which, :, low:high].astype(F32)
        return value + crossed_ref[which, :, low:high].astype(F32)

    if own_norm:
        hidden_ref, norm_ref = rest[-2:]
        squares = jnp.sum(total(0, width, width + 128), axis=1, keepdims=True)
        norm = lax.rsqrt(squares / model + 1e-06)
        norm_ref[...] = jnp.broadcast_to(norm, norm_ref.shape)
    else:
        hidden_ref = rest[-1]
        norm = rest[0][:, 0:1]
    gate = total(0, 0, width) * norm
    up = total(1, 0, width) * norm
    hidden_ref[...] = (gate / (1.0 + jnp.exp(-gate)) * up).astype(BF16)


def activate(model, width, keep, got, crossed, norm, *behind):
    high = keep.shape[1]
    shapes = [jax.ShapeDtypeStruct((high, width), BF16)]
    if norm is None:
        shapes.append(jax.ShapeDtypeStruct((high, 128), F32))
    ins = [keep, got, crossed] + ([] if norm is None else [norm]) + list(behind)
    result = pl.pallas_call(
        functools.partial(activate_kernel, model, width, norm is None),
        out_shape=shapes,
        compiler_params=params(),
        cost_estimate=cost(20 * high * width, 14 * high * width, high * width),
    )(*ins)
    return result if norm is None else (result[0], norm)


def down_kernel(width, slots, has_start, last, scalars, *refs):
    hidden = refs[0:4]
    weight_ref = refs[4]
    rest = list(refs[5:])
    start_ref = rest.pop(0) if has_start else None
    acc, packed = rest[-2], rest[-1]
    outs = rest[:-2]
    step = pl.program_id(0)
    depth = weight_ref.shape[0]
    high = hidden[0].shape[0]
    steps = pl.num_programs(0)

    @pl.when(step == 0)
    def begin():
        if width % depth:
            packed[...] = jnp.zeros_like(packed)
        for place in range(4):
            packed[place * high : (place + 1) * high, 0:width] = hidden[place][...]
        if has_start:
            acc[...] = start_ref[...]
        else:
            acc[...] = jnp.zeros_like(acc)

    def add(weight):
        if packed.shape[1] == depth:
            part = packed[...]
        else:
            part = packed[:, pl.ds(pl.multiple_of(step * depth, depth), depth)]
        term = jnp.dot(part, weight, preferred_element_type=F32)
        acc[...] += term.reshape(acc.shape)

    if width % depth:

        @pl.when(step < steps - 1)
        def inner():
            add(weight_ref[...])

        @pl.when(step == steps - 1)
        def edge():
            row = lax.broadcasted_iota(jnp.int32, weight_ref.shape, 0)
            add(jnp.where(row < width % depth, weight_ref[...], jnp.zeros_like(weight_ref)))
    else:
        add(weight_ref[...])

    @pl.when(step == steps - 1)
    def finish():
        if not last:
            outs[0][...] = acc[...]
            return
        rows = high // slots
        for k in range(4):
            place = swapped_bits(scalars[5] ^ k)
            block = acc[place]
            for s in range(slots):
                out = outs[k * slots + s]
                out[...] = block[s * rows : (s + 1) * rows].astype(out.dtype)


def down(scalars, hidden, down_weight, start, slots, last):
    high, width = hidden[0].shape
    cols = down_weight.shape[1]
    tile, steps = width, 1
    rows = high // slots
    ins = [whole((high, width))] * 4 + [pl.BlockSpec((tile, cols), lambda i, s: (i, 0))]
    args = list(hidden) + [down_weight]
    if start is not None:
        ins.append(whole((4, high, cols)))
        args.append(start)
    if last:
        shapes = [
            jax.ShapeDtypeStruct((rows, cols), F32 if s == 0 else BF16)
            for k in range(4)
            for s in range(slots)
        ]
    else:
        shapes = [jax.ShapeDtypeStruct((4, high, cols), F32)]
    return pl.pallas_call(
        functools.partial(down_kernel, width, slots, start is not None, last),
        grid_spec=pltpu.PrefetchScalarGridSpec(
            num_scalar_prefetch=1,
            grid=(steps,),
            in_specs=ins,
            out_specs=[whole(shape.shape) for shape in shapes],
            scratch_shapes=[
                pltpu.VMEM((4, high, cols), F32),
                pltpu.VMEM((4 * high, steps * tile), BF16),
            ],
        ),
        out_shape=shapes,
        compiler_params=params(),
        cost_estimate=cost(8 * high * width * cols, 2 * width * cols),
    )(scalars, *args)


def to_core(x):
    return lax.ppermute(x, "ffn", [(i, i ^ 1) for i in range(4)])


def to_x(x):
    return lax.ppermute(x, "ffn", [(i, i ^ 2) for i in range(4)])


def to_z(x, k):
    return lax.ppermute(x, "tp", [(i, i ^ k) for i in range(4)])


def to_y(x):
    return lax.ppermute(x, "grp", [(0, 1), (1, 0)])


def cut(total):
    return [(0, SPLIT), (SPLIT, total - SPLIT)]


def body(
    queries,
    new_kv,
    kv_cache,
    lengths,
    prefixes,
    resid,
    out_weight,
    gain,
    gate_weight,
    up_weight,
    down_weight,
):
    span = queries.shape[0]
    local_kv = new_kv.shape[2] // DH
    cache_len = kv_cache.shape[2]
    groups = lax.axis_size("grp")
    tp_size = lax.axis_size("tp")
    g, t, f = lax.axis_index("grp"), lax.axis_index("tp"), lax.axis_index("ffn")
    core = f & 1
    length = lengths[0]
    rows = span // tp_size
    model = gain.shape[0] * lax.axis_size("ffn")
    usable = jnp.clip(prefixes[0] - f * cache_len, 0, cache_len)
    first = (f == 0).astype(jnp.int32)
    scalars = jnp.stack([core, usable, length, first, t, t ^ f]).astype(jnp.int32)
    scalars = lax.optimization_barrier(scalars)
    sent, kept, sent_lse, kept_lse = attention(scalars, queries, kv_cache, new_kv)
    got, got_lse = to_core(sent), to_core(sent_lse)
    kept, kept_lse = combine(kept, got, kept_lse, got_lse, False)
    (out_held,), mark, kept = fetch([out_weight], [(0, out_weight.shape[0])], kept)
    got, got_lse = to_x(kept), to_x(kept_lse)
    (mine,) = combine(kept, got, kept_lse, got_lse, True, mark)
    other = to_core(mine)

    terms = list(project(scalars, mine, other, out_held, tp_size))
    chunks = cut(gate_weight.shape[1])
    pair = [gate_weight.T, up_weight.T]
    (gate0, up0, gate1), mark, terms[1] = fetch(
        pair + pair[:1], [chunks[0], chunks[0], chunks[1]], terms[1]
    )
    passed = [to_z(terms[k], k) for k in (1, 3, 2)]
    h1 = add_residual(scalars, resid, terms[0], passed, mark)

    natural = g ^ jnp.arange(groups, dtype=jnp.int32)
    by_z = [h1, to_z(h1, 1), to_z(h1, 2)]
    across = None
    if groups == 2:
        by_z[2], across = lax.optimization_barrier((by_z[2], to_y(h1)))
    by_z.append(to_z(by_z[2], 1))
    (up1,), mark, by_z[1] = fetch(pair[1:], chunks[1:], by_z[1])
    held = [(gate0, up0), (gate1, up1)]
    sources = []
    for part in by_z:
        if groups == 2:
            sources += [part, to_y(part) if sources else across]
        else:
            everyone = jnp.take(lax.all_gather(part, "grp"), natural, axis=0)
            sources += [everyone[s] for s in range(groups)]
    scaled, squares = scale_rows(scalars, sources, gain[None, :], mark)

    first, second = (width for begin, width in chunks)
    keep0, cross, side, far_side = gate_up(scaled, *held[0], first, squares)
    cross = (cross.astype(F32) + to_core(far_side).astype(F32)).astype(BF16)
    got0 = to_core(side)
    scaled, cross = lax.optimization_barrier((scaled, cross))
    crossed0 = to_x(cross)
    keep1, cross, side, far_side = gate_up(scaled, *held[1], second)
    got, crossed0 = lax.optimization_barrier((to_core(far_side), crossed0))
    cross = (cross.astype(F32) + got.astype(F32)).astype(BF16)
    got1 = to_core(side)
    held, mark, cross = fetch([down_weight] * 2, chunks, cross)
    crossed1 = to_x(cross)
    hidden, norm = activate(model, first, keep0, got0, crossed0, None, mark)
    over, near = to_x(hidden), to_core(hidden)
    later, norm = activate(model, second, keep1, got1, crossed1, norm, hidden)
    far = to_x(later)
    over, later = lax.optimization_barrier((over, later))
    pieces = [hidden, over, near, to_core(over)]
    (total,) = down(scalars, pieces, held[0], None, groups, False)
    far, total = lax.optimization_barrier((far, total))
    pieces = [later, far, to_core(later), to_core(far)]
    result = down(scalars, pieces, held[1], total, groups, True)

    chunk_sums = []
    for k in range(4):
        own = result[k * groups]
        others = result[k * groups + 1 : (k + 1) * groups]
        if groups == 2:
            chunk_sums.append((own, others[0]))
        else:
            stacked = jnp.stack([own.astype(BF16)] + list(others))
            stacked = jnp.take(stacked, natural, axis=0)
            moved = lax.all_to_all(stacked, "grp", split_axis=0, concat_axis=0, tiled=True)
            chunk_sums.append(jnp.sum(moved.astype(F32), axis=0))
    parts = [h1]
    for k in (2, 3, 1, 0):
        if groups == 2:
            own, away = chunk_sums[k]
            away = to_y(away)
            if k == 0:
                parts += [own, away]
                continue
            value = own + away.astype(F32)
        else:
            value = chunk_sums[k]
        parts.append(value if k == 0 else to_z(value.astype(BF16), k))
    total = sum(part.astype(F32) for part in parts)
    live = t * rows + jnp.arange(rows, dtype=jnp.int32) < length
    return jnp.where(live[:, None], total, 0.0).astype(BF16)


def merged(x, axis, combine):
    everything = jax.tree.map(lambda part: lax.all_gather(part, axis), x)
    leading = jax.tree.map(lambda part: part[0], everything)

    def hop(k, so_far):
        return combine(so_far, jax.tree.map(lambda part: part[k], everything))

    return lax.fori_loop(1, lax.axis_size(axis), hop, leading)


def combine_parts(first, second):
    top = jnp.maximum(first[0], second[0])
    left = jnp.exp(first[0] - top)
    right = jnp.exp(second[0] - top)
    total = first[1] * left + second[1] * right
    values = first[2] * left[..., None] + second[2] * right[..., None]
    return (top, total, values)


def general_body(
    queries,
    new_kv,
    kv_cache,
    lengths,
    prefixes,
    resid,
    out_weight,
    gain,
    gate_weight,
    up_weight,
    down_weight,
):
    span, qcols = queries.shape
    kcols = new_kv.shape[2]
    local_kv = kcols // DH
    group = qcols // DH // local_kv
    cache_len = kv_cache.shape[2]
    length = lengths[0]
    model = gain.shape[0] * lax.axis_size("ffn")
    prefix = prefixes[0]
    width_index = lax.axis_index("ffn")
    shard_start = width_index * cache_len
    query_heads = (
        queries.reshape(span, local_kv, group, DH)
        .transpose(1, 2, 0, 3)
        .reshape(local_kv, group * span, DH)
    )
    row_pos = jnp.tile(jnp.arange(span, dtype=jnp.int32), group)
    inv_scale = 1.0 / math.sqrt(DH)

    def update(state, keys, values, valid):
        top, total, acc = state
        scores = (
            jnp.einsum("hrd,hkd->hrk", query_heads, keys, preferred_element_type=jnp.float32)
            * inv_scale
        )
        scores = jnp.where(valid[None], scores, NEGATIVE)
        new_top = jnp.maximum(top, jnp.max(scores, axis=-1))
        probs = jnp.where(valid[None], jnp.exp(scores - new_top[..., None]), 0.0)
        factor = jnp.exp(top - new_top)
        total = total * factor + jnp.sum(probs, axis=-1)
        acc = acc * factor[..., None] + jnp.einsum(
            "hrk,hkd->hrd", probs, values.astype(jnp.float32)
        )
        return (new_top, total, acc)

    block = math.gcd(512, cache_len)
    blocks = cache_len // block
    cache_keys = kv_cache[0, 0].reshape(blocks, block, local_kv, DH).transpose(0, 2, 1, 3)
    cache_values = kv_cache[1, 0].reshape(blocks, block, local_kv, DH).transpose(0, 2, 1, 3)
    rows = group * span
    start_state = (
        jnp.full((local_kv, rows), NEGATIVE, jnp.float32),
        jnp.zeros((local_kv, rows), jnp.float32),
        jnp.zeros((local_kv, rows, DH), jnp.float32),
    )

    def cache_step(state, items):
        keys, values, index = items
        positions = shard_start + index * block + jnp.arange(block, dtype=jnp.int32)
        valid = jnp.broadcast_to((positions < prefix)[None, :], (rows, block))
        return (update(state, keys, values, valid), None)

    state, unused = lax.scan(
        cache_step, start_state, (cache_keys, cache_values, jnp.arange(blocks, dtype=jnp.int32))
    )
    block_keys = new_kv[0].reshape(span, local_kv, DH).transpose(1, 0, 2)
    block_values = new_kv[1].reshape(span, local_kv, DH).transpose(1, 0, 2)
    slots = jnp.arange(span, dtype=jnp.int32)[None, :]
    new_valid = (slots < length) & (slots <= row_pos[:, None]) & (width_index == 0)
    state = update(state, block_keys, block_values, new_valid)
    top, total, acc = merged(state, "ffn", combine_parts)
    heads = acc / total[..., None]
    attn = (
        heads.reshape(local_kv, group, span, DH)
        .transpose(2, 0, 1, 3)
        .reshape(span, qcols)
        .astype(jnp.bfloat16)
    )
    partial_value = jnp.dot(attn, out_weight, preferred_element_type=jnp.float32)
    summed = lax.psum(partial_value, "tp")
    h1 = (summed + resid.astype(jnp.float32)).astype(jnp.bfloat16)
    all_rows = lax.all_gather(h1, "grp", axis=0, tiled=True)
    rows_f = all_rows.astype(jnp.float32)
    squares = jnp.sum(rows_f * rows_f, axis=1)
    scaled = (rows_f * gain.astype(jnp.float32)[None, :]).astype(jnp.bfloat16)
    gate = jnp.dot(scaled, gate_weight, preferred_element_type=jnp.float32)
    upper = jnp.dot(scaled, up_weight, preferred_element_type=jnp.float32)
    rows_here = span // lax.axis_size("tp")
    gate, upper, squares = lax.psum((gate, upper, squares), "ffn")
    inv_rms = lax.rsqrt(squares / model + 1e-06)
    hidden = (jax.nn.silu(gate * inv_rms[:, None]) * (upper * inv_rms[:, None])).astype(
        jnp.bfloat16
    )
    down_rows = lax.psum_scatter(
        jnp.dot(hidden, down_weight, preferred_element_type=jnp.float32),
        ("grp", "tp"),
        scatter_dimension=0,
        tiled=True,
    )
    row_start = lax.axis_index("tp") * rows_here
    own = lax.dynamic_slice_in_dim(h1, row_start, rows_here, 0)
    live = row_start + jnp.arange(rows_here, dtype=jnp.int32) < length
    return jnp.where(live[:, None], own.astype(jnp.float32) + down_rows, 0.0).astype(jnp.bfloat16)


def solution(mesh):
    sizes = tuple(mesh.shape[axis] for axis in ("grp", "tp", "ffn"))
    return jax.shard_map(
        body if sizes == (2, 4, 4) else general_body,
        mesh=mesh,
        in_specs=(
            P("grp", "tp"),
            P(None, "grp", "tp"),
            P(None, "grp", "ffn", "tp"),
            P("grp"),
            P("grp"),
            P("grp", "ffn"),
            P("tp", "ffn"),
            P("ffn"),
            P("ffn", ("grp", "tp")),
            P("ffn", ("grp", "tp")),
            P(("grp", "tp"), "ffn"),
        ),
        out_specs=P(("grp", "tp"), "ffn"),
        check_vma=False,
    )
```
